128 devices in a mesh: fsdp: 16 (over y, z_hi, core), tp: 8 (over x, z_lo).
Axes of the slice: x: 4, y: 4, z: 4 (z_hi: 2, z_lo: 2; z = z_hi * 2 + z_lo), core: 2. Of those that a mesh axis runs over, the one named last changes fastest.
Arguments:
- tokens: bfloat16 [16384, 2048], P(('fsdp', 'tp')), may hold values from -6 to 6
- seq_lens: int32 [16, 8], P('fsdp'), may hold values from 0 to 1024, as said below
- ln1_gain: bfloat16 [2048], P('fsdp'), may hold values from 0.25 to 1.75
- ln1_bias: bfloat16 [2048], P('fsdp'), may hold values from -3 to 3
- w_qkv: bfloat16 [2048, 3, 2048], P('fsdp', None, 'tp'), may hold values from -0.125 to 0.125
- b_qkv: bfloat16 [3, 32, 64], P(None, 'tp', 'fsdp'), may hold values from -3 to 3
- w_out: bfloat16 [2048, 2048], P('tp', 'fsdp'), may hold values from -0.5 to 0.5
- ln2_gain: bfloat16 [2048], P('fsdp'), may hold values from 0.25 to 1.75
- ln2_bias: bfloat16 [2048], P('fsdp'), may hold values from -3 to 3
- w_gate: bfloat16 [2048, 5632], P('fsdp', 'tp'), may hold values from -0.125 to 0.125
- w_up: bfloat16 [2048, 5632], P('fsdp', 'tp'), may hold values from -0.125 to 0.125
- w_down: bfloat16 [5632, 2048], P('tp', 'fsdp'), may hold values from -0.078125 to 0.078125
- cotangent: bfloat16 [16384, 2048], P(('fsdp', 'tp')), may hold values from -6 to 6
Outputs:
- output: bfloat16 [16384, 2048], P(('fsdp', 'tp'))
- d_tokens: float32 [16384, 2048], P(('fsdp', 'tp'))
- d_ln1_gain: float32 [2048], P('fsdp')
- d_ln1_bias: float32 [2048], P('fsdp')
- d_w_qkv: float32 [2048, 3, 2048], P('fsdp', None, 'tp')
- d_b_qkv: float32 [3, 32, 64], P(None, 'tp', 'fsdp')
- d_w_out: float32 [2048, 2048], P('tp', 'fsdp')
- d_ln2_gain: float32 [2048], P('fsdp')
- d_ln2_bias: float32 [2048], P('fsdp')
- d_w_gate: float32 [2048, 5632], P('fsdp', 'tp')
- d_w_up: float32 [2048, 5632], P('fsdp', 'tp')
- d_w_down: float32 [5632, 2048], P('tp', 'fsdp')
The draws below stay inside these ranges and needn't reach their ends.
Inputs may be any that keep to these rules, and one draw needn't show every extreme that they name: `seq_lens`: each row lists the lengths of the sequences packed in order into the 1024 slots of one index of fsdp and sums to 1024; a zero is an empty entry; in one row a single sequence fills all 1024 slots.
All inputs are finite; a program needn't handle non-finite values.
Results may differ from the reference program's by a relative error of at most 0.035.
Values may be sent and summed in bfloat16 or wider, within the bound.
A program may use at most 192 MiB of HBM per device.

```python
import math
import jax
import jax.numpy as jnp
from jax import lax

D = 2048
HEADS = 32
HEAD_DIM = 64
FF = 5632
ROT = 16
SEQS = 8
GROUP = 1024
TOKENS = 16384
N_FSDP = 16
N_TP = 8


def draw_seq_lens(key, part):
    key = jax.random.fold_in(key, 11)
    cut_key, row_key = jax.random.split(key)
    cuts = jnp.sort(jax.random.randint(cut_key, (N_FSDP, SEQS - 1), 0, GROUP + 1), axis=1)
    zero_col = jnp.zeros((N_FSDP, 1), jnp.int32)
    full_col = jnp.full((N_FSDP, 1), GROUP, jnp.int32)
    edges = jnp.concatenate([zero_col, cuts.astype(jnp.int32), full_col], axis=1)
    lengths = edges[:, 1:] - edges[:, :-1]
    chosen = jax.random.randint(row_key, (), 0, N_FSDP)
    single = jnp.concatenate([full_col, jnp.zeros((N_FSDP, SEQS - 1), jnp.int32)], axis=1)
    picked = jnp.arange(N_FSDP)[:, None] == chosen
    return jnp.where(picked, single, lengths).astype(jnp.int32)


def steps_of(key, dims, cuts, low, high):
    def one(dim, shards_of):
        heights = jax.random.uniform(jax.random.fold_in(jax.random.fold_in(key, 6), dim), (shards_of,), jnp.float32, low / len(cuts), high / len(cuts))
        return jnp.repeat(jnp.exp(heights), dims[dim] // shards_of).reshape((-1,) + (1,) * (len(dims) - dim - 1))

    gain = one(*cuts[0])
    for cut in cuts[1:]:
        gain = gain * one(*cut)
    return gain


def bell_draw(rng, dims, scale, bound, cuts=(), kind=jnp.bfloat16):
    entries = jax.random.normal(rng, dims, jnp.float32) * scale
    if len(cuts) > 0:
        entries = steps_of(rng, dims, cuts, -0.22, 0.18) * entries
    return jnp.clip(entries, min=-bound, max=bound).astype(kind)


def setup_inputs(seed: int = 0) -> dict:
    seeds = jax.random.split(jax.random.key(seed), 14)
    tokens = bell_draw(seeds[0], (TOKENS, D), 1.0, 6.0, ((0, 128),))
    seq_lens = draw_seq_lens(jax.random.fold_in(seeds[13], 71), 0)
    ln1_gain = jnp.clip(1.0 + 0.15 * jax.random.normal(seeds[2], (D,), jnp.float32), 0.25, 1.75).astype(jnp.bfloat16)
    ln1_bias = bell_draw(seeds[3], (D,), 0.5, 3.0, ((0, 16),))
    w_qkv = bell_draw(seeds[4], (D, 3, D), D ** -0.5, 0.125, ((0, 16), (2, 8)))
    b_qkv = bell_draw(seeds[5], (3, HEADS, HEAD_DIM), 0.5, 3.0, ((1, 8), (2, 16)))
    w_out = bell_draw(seeds[6], (D, D), (D // 16) ** -0.5, 0.5, ((0, 8), (1, 16)))
    ln2_gain = jnp.clip(1.0 + 0.15 * jax.random.normal(seeds[7], (D,), jnp.float32), 0.25, 1.75).astype(jnp.bfloat16)
    ln2_bias = bell_draw(seeds[8], (D,), 0.5, 3.0, ((0, 16),))
    w_gate = bell_draw(seeds[9], (D, FF), D ** -0.5, 0.125, ((0, 16), (1, 8)))
    w_up = bell_draw(seeds[10], (D, FF), D ** -0.5, 0.125, ((0, 16), (1, 8)))
    w_down = bell_draw(seeds[11], (FF, D), FF ** -0.5, 0.078125, ((0, 8), (1, 16)))
    cotangent = bell_draw(seeds[12], (TOKENS, D), 1.0, 6.0, ((0, 128),))
    return dict(tokens=tokens, seq_lens=seq_lens, ln1_gain=ln1_gain, ln1_bias=ln1_bias, w_qkv=w_qkv, b_qkv=b_qkv, w_out=w_out, ln2_gain=ln2_gain, ln2_bias=ln2_bias, w_gate=w_gate, w_up=w_up, w_down=w_down, cotangent=cotangent)


@jax.custom_vjp
def low(v):
    return lax.optimization_barrier(v.astype(jnp.bfloat16)).astype(jnp.float32)

@jax.custom_vjp
def low_back(v):
    return v

def low_keep(v):
    return (low(v), None)

def low_pass(kept, grad):
    return (grad,)

def back_keep(v):
    return (v, None)

def back_low(kept, grad):
    return (low(grad),)
low.defvjp(low_keep, low_pass)
low_back.defvjp(back_keep, back_low)
norm_eps = 1e-05
rope_base = 10000.0
masked_value = -1e+30

def layer_norm(values, gain_row, offset_row):
    center = values - lax.optimization_barrier(jnp.mean(values, axis=-1, keepdims=True))
    spread = lax.optimization_barrier(jnp.mean(center * center, axis=-1, keepdims=True))
    return center * lax.rsqrt(spread + norm_eps) * gain_row + offset_row

def slot_tables(lengths, total_rows):
    slot_ids = jnp.arange(total_rows, dtype=jnp.int32)
    seq_ends = jnp.cumsum(lengths, dtype=jnp.int32)
    before = (seq_ends[None, :] <= slot_ids[:, None]).astype(jnp.int32)
    segment = lax.optimization_barrier(jnp.sum(before, axis=1, dtype=jnp.int32))
    seq_start = lax.optimization_barrier(jnp.sum(before * lengths[None, :], axis=1, dtype=jnp.int32))
    return (segment, slot_ids - seq_start)

def rotate(values, position, rot_dims, direction):
    half_dims = rot_dims // 2
    frequency = jnp.exp(jnp.arange(half_dims, dtype=jnp.float32) * (-2.0 * math.log(rope_base) / rot_dims))
    angles = position.astype(jnp.float32)[:, None] * frequency[None, :]
    cosine = jnp.cos(angles)[:, None, :]
    sine_part = direction * jnp.sin(angles)[:, None, :]
    first_half = values[..., :half_dims]
    second = values[..., half_dims:rot_dims]
    return jnp.concatenate([first_half * cosine - second * sine_part, second * cosine + first_half * sine_part, values[..., rot_dims:]], axis=-1)

def group_attention(packed):
    qkv_group, lengths = packed
    total_rows = qkv_group.shape[0]
    segment, position = slot_tables(lengths, total_rows)
    slot_ids = jnp.arange(total_rows, dtype=jnp.int32)
    allowed = (segment[:, None] == segment[None, :]) & (slot_ids[None, :] <= slot_ids[:, None])
    queries = low(rotate(qkv_group[:, 0], position, ROT, 1.0))
    key_rows = low(rotate(qkv_group[:, 1], position, ROT, 1.0))
    value_rows = low(qkv_group[:, 2])
    scores = jnp.einsum('qhe,khe->hqk', queries, key_rows, precision=lax.Precision.HIGHEST) * HEAD_DIM ** (-0.5)
    scores = low_back(scores)
    scores = jnp.where(allowed[None], scores, masked_value)
    highest = lax.optimization_barrier(jnp.max(scores, axis=-1, keepdims=True))
    weights = jnp.exp(scores - highest)
    probability = low(weights / lax.optimization_barrier(jnp.sum(weights, axis=-1, keepdims=True)))
    mixed_rows = jnp.einsum('hqk,khe->qhe', probability, value_rows, precision=lax.Precision.HIGHEST)
    return low_back(low(mixed_rows)).reshape(total_rows, HEADS * HEAD_DIM)

def reference(tokens, seq_lens, ln1_gain, ln1_bias, w_qkv, b_qkv, w_out, ln2_gain, ln2_bias, w_gate, w_up, w_down, cotangent):
    precise = lax.Precision.HIGHEST
    width_block = D // N_TP
    head_block = HEADS // N_TP
    ff_block = FF // N_TP

    def forward(inputs, gain_one, shift_one, qkv_weight, qkv_bias, out_weight, gain_two, shift_two, gate_weight, up_weight, down_weight):
        normed = low(layer_norm(inputs, gain_one, shift_one))
        pieces = []
        for block in range(N_TP):
            normed_copy = low_back(normed)
            weight_block = qkv_weight[:, :, block * width_block:(block + 1) * width_block].reshape(D, 3 * width_block)
            bias_block = qkv_bias[:, block * head_block:(block + 1) * head_block].reshape(3 * width_block)
            piece = jnp.dot(normed_copy, weight_block, precision=precise) + bias_block
            pieces.append(low_back(piece).reshape(TOKENS, 3, head_block, HEAD_DIM))
        projected_rows = jnp.concatenate(pieces, axis=2).reshape(N_FSDP, GROUP, 3, HEADS, HEAD_DIM)
        attended = lax.map(jax.checkpoint(group_attention), (projected_rows, seq_lens)).reshape(TOKENS, D)
        branch = jnp.zeros((TOKENS, D), jnp.float32)
        for block in range(N_TP):
            rows = slice(block * width_block, (block + 1) * width_block)
            branch = branch + low(jnp.dot(attended[:, rows], out_weight[rows], precision=precise))
        middle = inputs + low_back(branch)
        normed_two = low(layer_norm(middle, gain_two, shift_two))
        down_sum = jnp.zeros((TOKENS, D), jnp.float32)
        for block in range(N_TP):
            units = slice(block * ff_block, (block + 1) * ff_block)
            normed_copy = low_back(normed_two)
            gate_value = low_back(jnp.dot(normed_copy, gate_weight[:, units], precision=precise))
            up_value = low_back(jnp.dot(normed_copy, up_weight[:, units], precision=precise))
            hidden = low(gate_value * jax.nn.sigmoid(gate_value) * up_value)
            down_sum = down_sum + low(jnp.dot(hidden, down_weight[units], precision=precise))
        return middle + low_back(down_sum)
    result, pullback = jax.vjp(forward, tokens.astype(jnp.float32), ln1_gain.astype(jnp.float32), ln1_bias.astype(jnp.float32), w_qkv.astype(jnp.float32), b_qkv.astype(jnp.float32), w_out.astype(jnp.float32), ln2_gain.astype(jnp.float32), ln2_bias.astype(jnp.float32), w_gate.astype(jnp.float32), w_up.astype(jnp.float32), w_down.astype(jnp.float32))
    gradients = pullback(cotangent.astype(jnp.float32))
    return (result.astype(jnp.bfloat16), gradients[0], gradients[1], gradients[2], gradients[3], gradients[4], gradients[5], gradients[6], gradients[7], gradients[8], gradients[9], gradients[10])
```

```python
import math

import jax
import jax.numpy as jnp
import numpy as np
from jax import lax
from jax.experimental import pallas as pl
from jax.experimental.pallas import tpu as pltpu
from jax.sharding import PartitionSpec as P

F32 = jnp.float32
BF16 = jnp.bfloat16
HEAD_DIM = 64
ROT = 16
EPS = 1e-05
ROPE_BASE = 10000.0
MASKED = -1e30
SCALE = HEAD_DIM**-0.5
ROWS_A = 1040
ROWS_Q = 784
ROWS_M = 704
MIB = 2**20


def nt(a, b):
    return lax.dot_general(a, b, (((1,), (1,)), ((), ())), preferred_element_type=F32)


def nn(a, b):
    return lax.dot_general(a, b, (((1,), (0,)), ((), ())), preferred_element_type=F32)


class Net:
    def __init__(self, send_sems, recv_sems, local_sems):
        f, t = lax.axis_index("fsdp"), lax.axis_index("tp")
        self.f, self.t = f, t
        self.x, self.zl = t // 2, lax.rem(t, 2)
        self.send_sems, self.recv_sems, self.local_sems = send_sems, recv_sems, local_sems
        self.started, self.pending, self.locals = 0, [], 0

    def tx(self, step, flip=0):
        zl = 1 - self.zl if flip else self.zl
        return lax.rem(self.x + step, 4) * 2 + zl

    def fy(self, f, step):
        return lax.rem(f + 4 * step, 16)

    def peer(self, name):
        if not isinstance(name, str):
            return name
        f, t = self.f, self.t
        core = f + 1 - 2 * lax.rem(f, 2)
        high = f + 2 - 4 * lax.rem(f // 2, 2)
        return {
            "xp": (f, self.tx(1)),
            "xm": (f, self.tx(3)),
            "zl": (f, self.tx(0, 1)),
            "zh": (high, t),
            "zo": (high, self.tx(0, 1)),
            "yp": (self.fy(f, 1), t),
            "ym": (self.fy(f, 3), t),
            "c": (core, t),
        }[name]

    def greet(self, names):
        barrier = pltpu.get_barrier_semaphore()
        for name in names:
            pl.semaphore_signal(
                barrier, inc=1, device_id=self.peer(name), device_id_type=pl.DeviceIdType.MESH
            )
        pl.semaphore_wait(barrier, len(names))

    def send(self, src, dst, name):
        k = self.started
        copy = pltpu.make_async_remote_copy(
            src_ref=src,
            dst_ref=dst,
            send_sem=self.send_sems.at[k],
            recv_sem=self.recv_sems.at[k],
            device_id=self.peer(name),
            device_id_type=pl.DeviceIdType.MESH,
        )
        copy.start()
        self.started += 1
        self.pending.append(copy)
        return copy

    def move(self, src, dst):
        copy = pltpu.make_async_copy(src, dst, self.local_sems.at[self.locals])
        copy.start()
        self.locals += 1
        return copy

    def settle(self, copies):
        for copy in copies:
            copy.wait_send()
        done = {id(copy) for copy in copies}
        self.pending = [copy for copy in self.pending if id(copy) not in done]

    def finish(self):
        for copy in self.pending:
            copy.wait_send()
        self.pending = []


class GatherTp:
    def __init__(self, net, src, buf):
        self.net, self.buf, self.src = net, buf, src
        half = src.shape[0] // 2
        self.lo, self.hi = pl.ds(0, half), pl.ds(half, half)

    def slot(self, step, flip=0):
        zl = 1 - self.net.zl if flip else self.net.zl
        return zl * 4 + lax.rem(self.net.x + step, 4)

    def pass_on(self, slot, rows, name):
        return self.net.send(self.buf.at[slot, rows], self.buf.at[slot, rows], name)

    def start(self):
        net, lo, hi = self.net, self.lo, self.hi
        own = self.slot(0)
        self.own = net.move(self.src, self.buf.at[own])
        self.xp_lo = net.send(self.src.at[lo], self.buf.at[own, lo], "xp")
        self.xm_hi = net.send(self.src.at[hi], self.buf.at[own, hi], "xm")
        self.xp_hi = net.send(self.src.at[hi], self.buf.at[own, hi], "xp")
        self.xm_lo = net.send(self.src.at[lo], self.buf.at[own, lo], "xm")

    def start_z(self):
        self.z = self.net.send(self.src, self.buf.at[self.slot(0)], "zl")

    def relay(self):
        lo, hi = self.lo, self.hi
        left, right = self.slot(3), self.slot(1)
        self.xp_lo.wait_recv()
        self.fwd_p = self.pass_on(left, lo, "xp")
        self.xm_hi.wait_recv()
        self.fwd_m = self.pass_on(right, hi, "xm")
        self.xp_hi.wait_recv()
        self.za_p = self.pass_on(left, hi, "zl")
        self.xm_lo.wait_recv()
        self.za_m = self.pass_on(right, lo, "zl")

    def relay_z(self):
        across = self.slot(0, 1)
        self.z.wait_recv()
        self.zb_p = self.pass_on(across, self.lo, "xp")
        self.zb_m = self.pass_on(across, self.hi, "xm")

    def relay_far(self):
        self.zb_p.wait_recv()
        self.fz_p = self.pass_on(self.slot(3, 1), self.lo, "xp")
        self.zb_m.wait_recv()
        self.fz_m = self.pass_on(self.slot(1, 1), self.hi, "xm")

    def plane(self):
        self.fwd_p.wait_recv()
        self.fwd_m.wait_recv()
        self.own.wait()

    def rest(self):
        for copy in (self.za_p, self.za_m, self.fz_p, self.fz_m):
            copy.wait_recv()


class GatherX:
    def __init__(self, net, src, buf):
        self.net, self.buf, self.src = net, buf, src
        self.half = src.shape[0] // 2

    def slot(self, step):
        return lax.rem(self.net.x + step, 4)

    def start(self):
        net, h = self.net, self.half
        lo, hi = pl.ds(0, h), pl.ds(h, h)
        own = self.slot(0)
        self.own = net.move(self.src, self.buf.at[own])
        self.xp_lo = net.send(self.src.at[lo], self.buf.at[own, lo], "xp")
        self.xm_hi = net.send(self.src.at[hi], self.buf.at[own, hi], "xm")
        self.xp_hi = net.send(self.src.at[hi], self.buf.at[own, hi], "xp")
        self.xm_lo = net.send(self.src.at[lo], self.buf.at[own, lo], "xm")

    def relay(self):
        net, h = self.net, self.half
        lo, hi = pl.ds(0, h), pl.ds(h, h)
        left, right = self.slot(3), self.slot(1)
        self.xp_lo.wait_recv()
        self.fwd_p = net.send(self.buf.at[left, lo], self.buf.at[left, lo], "xp")
        self.xm_hi.wait_recv()
        self.fwd_m = net.send(self.buf.at[right, hi], self.buf.at[right, hi], "xm")

    def near(self):
        self.xp_hi.wait_recv()
        self.xm_lo.wait_recv()

    def far(self):
        self.fwd_p.wait_recv()
        self.fwd_m.wait_recv()


class GatherW:
    def __init__(self, net, src, buf, wide, offset=0):
        self.net, self.src, self.buf, self.wide, self.offset = net, src, buf, wide, offset
        self.half = src.shape[0] // 32 * 16
        f = net.f
        high = f + 2 - 4 * lax.rem(f // 2, 2)
        self.sources = [((0, f), None), ((0, high), "zh")]
        if wide:
            self.sources += [((1, f), "zl"), ((1, high), "zo")]

    def at(self, key, step, rows=None):
        flip, f = key
        f = self.net.fy(f, step)
        start, size = (0, self.src.shape[0]) if rows is None else rows
        rows = pl.ds(self.offset + start, size)
        if self.wide:
            side = 1 - self.net.zl if flip else self.net.zl
            place = (f,) if len(self.buf.shape) == 4 else (f // 4, lax.rem(f // 2, 2), lax.rem(f, 2))
            return self.buf.at[(side, *place, rows)]
        return self.buf.at[f, rows]

    def pass_on(self, key, step, name, rows=None, src=None):
        here = self.at(key, step, rows)
        return self.net.send(here if src is None else src, here, name)

    def start(self):
        net, src = self.net, self.src
        own = (0, net.f)
        self.own = net.move(src, self.at(own, 0))
        self.by_z = [
            self.pass_on(own, 0, name, src=src) for _, name in self.sources if name is not None
        ]
        self.by_y = [(self.pass_on(own, 0, "yp", src=src), self.pass_on(own, 0, "ym", src=src))]
        self.by_c = [self.pass_on(own, 0, "c", src=src)]
        self.by_y2 = []

    def relay_z(self):
        for copy, (key, _) in zip(self.by_z, self.sources[1:]):
            copy.wait_recv()
            self.by_y.append((self.pass_on(key, 0, "yp"), self.pass_on(key, 0, "ym")))
            self.by_c.append(self.pass_on(key, 0, "c"))

    def relay_y(self, i):
        key, h = self.sources[i][0], self.half
        up, down = self.by_y[i]
        rows = self.src.shape[0]
        up.wait_recv()
        fwd_up = self.pass_on(key, 3, "yp", (0, h))
        down.wait_recv()
        fwd_down = self.pass_on(key, 1, "ym", (h, rows - h))
        self.by_c.append(self.pass_on(key, 3, "c"))
        self.by_c.append(self.pass_on(key, 1, "c"))
        self.by_y2.append((fwd_up, fwd_down))

    def relay_far(self, i):
        for copy in self.by_y2[i]:
            copy.wait_recv()
        self.by_c.append(self.pass_on(self.sources[i][0], 2, "c"))

    def finish(self):
        self.own.wait()
        for copy in self.by_c:
            copy.wait_recv()


def norm_rows(x, gain, bias):
    center = x - jnp.mean(x, axis=-1, keepdims=True)
    spread = jnp.mean(center * center, axis=-1, keepdims=True)
    return center * lax.rsqrt(spread + EPS) * gain + bias


def position_tables(lens_ref, begin_ref, cos_ref, sin_ref):
    rows = begin_ref.shape[0]
    slot = lax.broadcasted_iota(jnp.int32, (rows, 128), 0)
    begin = jnp.zeros((rows, 128), jnp.int32)
    end = jnp.int32(0)
    for i in range(lens_ref.shape[1]):
        length = lens_ref[0, i]
        end = end + length
        begin = begin + jnp.where(slot >= end, length, 0)
    begin_ref[...] = begin
    lane = lax.rem(lax.broadcasted_iota(jnp.int32, (1, 128), 1), HEAD_DIM)
    which = lax.rem(lane, ROT // 2)
    frequency = jnp.zeros((1, 128), F32)
    for j in range(ROT // 2):
        value = float(np.exp(np.float32(j) * np.float32(-2.0 * math.log(ROPE_BASE) / ROT)))
        frequency = jnp.where(which == j, value, frequency)
    angle = (slot - begin).astype(F32) * frequency
    turns = jnp.floor(angle * (2.0 / math.pi) + 0.5)
    r = angle - turns * 1.5703125 - turns * 4.837512969970703125e-4 - turns * 7.54978995489188216e-8
    z = r * r
    sine = ((-1.9515295891e-4 * z + 8.3321608736e-3) * z - 1.6666654611e-1) * z * r + r
    cosine = (
        ((2.443315711809948e-5 * z - 1.388731625493765e-3) * z + 4.166664568298827e-2) * z * z
        - 0.5 * z
        + 1.0
    )
    quadrant = turns - 4.0 * jnp.floor(turns * 0.25)
    odd = (quadrant == 1.0) | (quadrant == 3.0)
    cos_all = jnp.where(odd, sine, cosine)
    cos_all = jnp.where((quadrant == 1.0) | (quadrant == 2.0), -cos_all, cos_all)
    sin_all = jnp.where(odd, cosine, sine)
    sin_all = jnp.where(quadrant >= 2.0, -sin_all, sin_all)
    cos_ref[...] = jnp.where(lane < ROT, cos_all, 1.0)
    sin_ref[...] = jnp.where(lane < ROT, sin_all, 0.0)


def turn(values, cos, sin, direction):
    lane = lax.rem(lax.broadcasted_iota(jnp.int32, (1, 256), 1), HEAD_DIM)
    cos = jnp.concatenate([cos, cos], axis=1)
    sin = jnp.concatenate([sin, sin], axis=1) * direction
    after = pltpu.roll(values, 256 - ROT // 2, 1)
    before = pltpu.roll(values, ROT // 2, 1)
    other = jnp.where(lane < ROT // 2, -after, before)
    return values * cos + other * sin


def head_mask(h):
    return lax.broadcasted_iota(jnp.int32, (1, 256), 1) // HEAD_DIM == h


def scores_of(q_block, keys, begin, first, h):
    rows, stop = q_block.shape[0], keys.shape[0]
    q_head = jnp.where(head_mask(h), q_block, jnp.zeros_like(q_block))
    scores = nt(q_head, keys)
    key_slot = lax.broadcasted_iota(jnp.int32, (rows, stop), 1)
    query_slot = lax.broadcasted_iota(jnp.int32, (rows, stop), 0) + first
    return jnp.where((key_slot >= begin) & (key_slot <= query_slot), scores, MASKED)


def flip_into(ref, first, source):
    columns = source.shape[1]
    for begin in range(0, columns, 128):
        end = min(begin + 128, columns)
        ref[first + begin : first + end] = source[:, begin:end].T


def k1_kernel(
    x_ref, lens_ref, small_ref, w_qkv, w_out, pack_g, cot_ref,
    normed_hbm, wa_hbm, wg_hbm, cotg_hbm, q_hbm, k_hbm, v_hbm, att_hbm,
    normed_ref, wa_ref, wg_ref, cotg_ref, q_ref, k_ref, v_ref, att_ref,
    pack_a, raw, gains, biases, begin_ref, cos_ref, sin_ref, send_sems, recv_sems, local_sems,
):
    net = Net(send_sems, recv_sems, local_sems)
    pack_a[0:16] = small_ref[...]
    for j in range(3):
        flip_into(pack_a, 16 + 256 * j, w_qkv.at[j])
    net.greet(["xp", "xm", "zl", "zh", "zo", "yp", "ym", "c"])
    tokens = GatherTp(net, x_ref, raw)
    wa = GatherW(net, pack_a, wa_ref, False)
    wo = GatherW(net, w_out, wa_ref, False, ROWS_Q)
    wg = GatherW(net, pack_g, wg_ref, True)
    cot = GatherX(net, cot_ref, cotg_ref)
    wa.start()
    tokens.start()
    position_tables(lens_ref, begin_ref, cos_ref, sin_ref)
    wa.relay_z()
    tokens.start_z()
    wa.relay_y(0)
    tokens.relay()
    wa.relay_far(0)
    wa.relay_y(1)
    wg.start()
    wa.relay_far(1)
    tokens.relay_z()
    wa.finish()
    stores = []
    for f in range(16):
        small = wa_ref[f, 0:16].astype(F32)
        gains[0:2, f * 128 : (f + 1) * 128] = small[0:2]
        biases[0:16, :] = small if f == 0 else biases[0:16, :] + small

    def project(side):
        def norm_some(i, carry):
            values = raw[side * 4 + i].astype(F32)
            normed_ref[i * 2 + side] = norm_rows(values, gains[0:1, :], gains[1:2, :]).astype(BF16)
            return carry

        lax.fori_loop(0, 4, norm_some, 0)

        def some_rows(i, carry):
            chunks = [2 * (2 * i + n) + side for n in range(2)]
            given = jnp.concatenate([normed_ref[chunk] for chunk in chunks], axis=0)
            rows = [pl.ds(pl.multiple_of(chunk * 128, 128), 128) for chunk in chunks]
            cos = jnp.concatenate([cos_ref[r] for r in rows], axis=0)
            sin = jnp.concatenate([sin_ref[r] for r in rows], axis=0)
            for j, out in enumerate((q_ref, k_ref, v_ref)):
                lines = slice(16 + 256 * j, 16 + 256 * (j + 1))
                total = nt(given, jnp.concatenate([wa_ref[f, lines] for f in range(16)], axis=1))
                total = total + jnp.concatenate([biases[4 + 2 * j : 5 + 2 * j], biases[5 + 2 * j : 6 + 2 * j]], axis=1)
                if j < 2:
                    total = turn(total, cos, sin, 1.0)
                for n in range(2):
                    out[rows[n]] = total[n * 128 : (n + 1) * 128].astype(BF16)
            return carry

        lax.fori_loop(0, 2, some_rows, 0)

    tokens.plane()
    wg.relay_y(0)
    project(net.zl)
    tokens.relay_far()
    wo.start()
    wg.relay_z()
    cot.start()
    wg.relay_far(0)
    tokens.rest()
    project(1 - net.zl)
    stores += [net.move(normed_ref, normed_hbm), net.move(q_ref, q_hbm)]
    stores += [net.move(k_ref, k_hbm), net.move(v_ref, v_hbm)]
    wg.relay_y(1)
    for block in range(4):
        first, stop = block * 256, (block + 1) * 256
        q_block = q_ref[first:stop] * jnp.asarray(SCALE, BF16)
        begin = begin_ref[first:stop, 0:1]
        mixed = jnp.zeros((256, 256), F32)
        for h in range(4):
            scores = scores_of(q_block, k_ref[0:stop], begin, first, h)
            weights = jnp.exp(scores - jnp.max(scores, axis=-1, keepdims=True))
            probs = (weights * (1.0 / jnp.sum(weights, axis=-1, keepdims=True))).astype(BF16)
            mixed = jnp.where(head_mask(h), nn(probs, v_ref[0:stop]), mixed)
        att_ref[first:stop] = mixed.astype(BF16)
        if block == 1:
            wg.relay_y(2)
            wo.relay_z()
        if block == 2:
            wg.relay_y(3)
            wg.relay_far(1)
            wo.relay_y(0)
    stores.append(net.move(att_ref, att_hbm))
    cot.relay()
    wo.relay_y(1)
    wg.relay_far(2)
    wg.relay_far(3)
    wo.relay_far(0)
    wo.relay_far(1)
    wg.finish()
    stores.append(net.move(wg_ref, wg_hbm))
    wo.finish()
    stores.append(net.move(wa_ref, wa_hbm))
    cot.own.wait()
    cot.near()
    cot.far()
    stores.append(net.move(cotg_ref, cotg_hbm))
    for copy in stores:
        copy.wait()
    net.finish()


def hbm(shape, dtype=BF16):
    return jax.ShapeDtypeStruct(shape, dtype)


VM = pl.BlockSpec(memory_space=pltpu.VMEM)
SM = pl.BlockSpec(memory_space=pltpu.SMEM)
AN = pl.BlockSpec(memory_space=pl.ANY)


def k1(x, lens, small, w_qkv, w_out, pack_g, cot):
    shapes = [
        (8, 128, 2048), (16, ROWS_A, 128), (2, 16, ROWS_M, 128), (4, 128, 2048),
        (1024, 256), (1024, 256), (1024, 256), (1024, 256),
    ]
    return pl.pallas_call(
        k1_kernel,
        out_shape=[hbm(s) for s in shapes],
        in_specs=[VM, SM, VM, VM, VM, VM, VM],
        out_specs=[AN] * 8,
        scratch_shapes=[pltpu.VMEM(s, BF16) for s in shapes + [(ROWS_Q, 128)]]
        + [
            pltpu.VMEM((8, 128, 2048), BF16),
            pltpu.VMEM((8, 2048), F32),
            pltpu.VMEM((16, 128), F32),
            pltpu.VMEM((1024, 128), jnp.int32),
            pltpu.VMEM((1024, 128), F32),
            pltpu.VMEM((1024, 128), F32),
            pltpu.SemaphoreType.DMA((160,)),
            pltpu.SemaphoreType.DMA((160,)),
            pltpu.SemaphoreType.DMA((16,)),
        ],
        compiler_params=pltpu.CompilerParams(
            collective_id=1, has_side_effects=True, vmem_limit_bytes=56 * MIB
        ),
        name="gather_project_attend",
    )(x, lens, small, w_qkv, w_out, pack_g, cot)


def small_rows(ln1_gain, ln1_bias, b_qkv, ln2_gain, ln2_bias):
    spread = jnp.zeros((3, 4, 16, 4), BF16)
    spread = lax.dynamic_update_slice(
        spread, b_qkv.reshape(3, 4, 1, 4), (0, 0, lax.axis_index("fsdp"), 0)
    ).reshape(6, 128)
    rows = lax.broadcasted_iota(jnp.int32, (16, 128), 0)
    small = jnp.pad(spread, ((4, 6), (0, 0)))
    for i, row in enumerate((ln1_gain, ln1_bias, ln2_gain, ln2_bias)):
        small = jnp.where(rows == i, row[None, :], small)
    return small


class ScatterTp:
    def __init__(self, net, parts, got, got_half):
        self.net, self.parts, self.got, self.got_half = net, parts, got, got_half
        half = parts.shape[1] // 2
        self.lo, self.hi = pl.ds(0, half), pl.ds(half, half)

    slot = GatherTp.slot

    def half_to(self, slot, rows, name, place):
        return self.net.send(self.parts.at[slot, rows], self.got_half.at[place], name)

    def add(self, slot, rows, *places):
        total = self.parts[slot, rows].astype(F32)
        for place in places:
            total = total + self.got_half[place].astype(F32)
        self.parts[slot, rows] = total.astype(BF16)

    def start_side(self):
        lo, hi = self.lo, self.hi
        self.zx2 = [self.half_to(self.slot(2, 1), lo, "xm", 0), self.half_to(self.slot(2, 1), hi, "xp", 1)]
        self.by_z = [self.half_to(self.slot(3, 1), hi, "zl", 2), self.half_to(self.slot(1, 1), lo, "zl", 4)]

    def start_plane(self):
        net, parts, lo, hi = self.net, self.parts, self.lo, self.hi
        far, left, right = self.slot(2), self.slot(3), self.slot(1)
        self.x2 = [self.half_to(far, hi, "xm", 6), self.half_to(far, lo, "xp", 7)]
        self.near_m = [net.send(parts.at[left, lo], self.got.at[1, lo], "xm")]
        self.near_p = [net.send(parts.at[right, hi], self.got.at[2, hi], "xp")]

    def relay_side(self):
        lo, hi = self.lo, self.hi
        self.zx2[0].wait_recv()
        self.add(self.slot(3, 1), lo, 0)
        self.across = [self.half_to(self.slot(3, 1), lo, "xm", 3)]
        self.zx2[1].wait_recv()
        self.add(self.slot(1, 1), hi, 1)
        self.across.append(self.half_to(self.slot(1, 1), hi, "xp", 5))

    def relay_across(self):
        across = self.slot(0, 1)
        self.across[0].wait_recv()
        self.add(across, self.lo, 3)
        self.across[1].wait_recv()
        self.add(across, self.hi, 5)
        self.z_own = self.net.send(self.parts.at[across], self.got.at[0], "zl")

    def relay_near(self):
        net, parts, lo, hi = self.net, self.parts, self.lo, self.hi
        left, right = self.slot(3), self.slot(1)
        self.by_z[0].wait_recv()
        self.x2[0].wait_recv()
        self.add(left, hi, 2, 6)
        self.near_m.append(net.send(parts.at[left, hi], self.got.at[1, hi], "xm"))
        self.by_z[1].wait_recv()
        self.x2[1].wait_recv()
        self.add(right, lo, 4, 7)
        self.near_p.append(net.send(parts.at[right, lo], self.got.at[2, lo], "xp"))

    def wait(self):
        self.z_own.wait_recv()
        for copy in self.near_p + self.near_m:
            copy.wait_recv()

    def total(self):
        total = self.parts[self.slot(0)].astype(F32)
        for i in range(3):
            total = total + self.got[i].astype(F32)
        return total


class ScatterX:
    def __init__(self, net, parts, got, got_half):
        self.net, self.parts, self.got, self.got_half = net, parts, got, got_half
        self.half = parts.shape[1] // 2

    slot = GatherX.slot

    def add(self, slot, rows, arrived):
        total = self.parts[slot, rows].astype(F32) + arrived[...].astype(F32)
        self.parts[slot, rows] = total.astype(BF16)

    def start_far(self):
        net, h, parts = self.net, self.half, self.parts
        far = self.slot(2)
        self.half_p = net.send(parts.at[far, pl.ds(0, h)], self.got_half.at[0], "xp")
        self.half_m = net.send(parts.at[far, pl.ds(h, h)], self.got_half.at[1], "xm")

    def start_near(self):
        net, h, parts = self.net, self.half, self.parts
        right, left = self.slot(1), self.slot(3)
        self.near_p = [net.send(parts.at[right, pl.ds(h, h)], self.got.at[0, pl.ds(h, h)], "xp")]
        self.near_m = [net.send(parts.at[left, pl.ds(0, h)], self.got.at[1, pl.ds(0, h)], "xm")]

    def relay_near(self):
        net, h, parts = self.net, self.half, self.parts
        right, left = self.slot(1), self.slot(3)
        self.half_p.wait_recv()
        self.add(right, pl.ds(0, h), self.got_half.at[0])
        self.near_p.append(net.send(parts.at[right, pl.ds(0, h)], self.got.at[0, pl.ds(0, h)], "xp"))
        self.half_m.wait_recv()
        self.add(left, pl.ds(h, h), self.got_half.at[1])
        self.near_m.append(net.send(parts.at[left, pl.ds(h, h)], self.got.at[1, pl.ds(h, h)], "xm"))

    def wait(self):
        for copy in self.near_p + self.near_m:
            copy.wait_recv()

    def total(self):
        total = self.parts[self.slot(0)].astype(F32)
        return total + self.got[0].astype(F32) + self.got[1].astype(F32)


def side_by_side(ref, lead, lines, slabs):
    return jnp.concatenate([ref[(*lead, f, lines)] for f in slabs], axis=1)


TILES = ((0, 256), (256, 512), (512, 704))


def k2_kernel(
    x_ref, att_ref, wa_hbm, wg_hbm, pack_u, pack_d, cot_ref, cotg_hbm,
    middle_hbm, gmid_ref, down_hbm, grads_hbm, ln2_ref,
    wo, small_ref, middle_ref, down_ref, parts, got8, got8_half, gains, n2_own, n2, wg, wu, wd, cotg, gate, up, ghid, hid, gg, gu, got4, got4_half, flipped,
    send_sems, recv_sems, local_sems,
):
    net = Net(send_sems, recv_sems, local_sems)
    net.greet(["xp", "xm", "zl", "zh", "zo", "yp", "ym", "c"])
    wug = GatherW(net, pack_u, wu, True)
    wdg = GatherW(net, pack_d, wd, True)
    wdg.start()
    first = [net.move(wa_hbm.at[:, pl.ds(784, 256)], wo), net.move(wa_hbm.at[:, pl.ds(0, 16)], small_ref)]
    moves = [net.move(wg_hbm, wg), net.move(cotg_hbm, cotg)]
    for copy in first:
        copy.wait()
    sum8 = ScatterTp(net, parts, got8, got8_half)

    def attention_out(side):
        rows = [att_ref[pl.ds(pl.multiple_of((2 * i + side) * 128, 128), 128)] for i in range(4)]
        rows = jnp.concatenate(rows, axis=0)
        for pair in range(8):
            weight = side_by_side(wo, (), slice(0, 256), (2 * pair, 2 * pair + 1))
            part = nn(rows, weight).astype(BF16).reshape(4, 128, 256)
            parts[pl.ds(side * 4, 4), :, pair * 256 : (pair + 1) * 256] = part

    attention_out(1 - net.zl)
    sum8.start_side()
    attention_out(net.zl)
    for f in range(16):
        small = small_ref[f].astype(F32)
        gains[0:2, f * 128 : (f + 1) * 128] = small[2:4]
    sum8.start_plane()
    sum8.relay_side()
    wdg.relay_z()
    wug.start()
    wdg.relay_y(0)
    sum8.relay_across()
    for i in range(1, 4):
        wdg.relay_y(i)
    wug.relay_z()
    sum8.relay_near()
    for i in range(4):
        wdg.relay_far(i)
    wug.relay_y(0)
    sum8.wait()
    middle = x_ref[...].astype(F32) + sum8.total()
    middle_ref[...] = middle
    n2_own[...] = norm_rows(middle, gains[0:1], gains[1:2]).astype(BF16)
    gather = GatherX(net, n2_own, n2)
    gather.start()
    stores = [net.move(middle_ref, middle_hbm)]
    for copy in moves:
        copy.wait()
    for i in range(1, 4):
        wug.relay_y(i)
    wdg.finish()

    def rows_of(slot):
        return pl.ds(slot * 128 if isinstance(slot, int) else pl.multiple_of(slot * 128, 128), 128)

    def grad_hidden(slots):
        given = jnp.concatenate([cotg[slot] for slot in slots], axis=0)
        for side in range(2):
            for a, b in TILES:
                value = nt(given, side_by_side(wd, (side,), slice(a, b), range(16))).astype(BF16)
                for i, slot in enumerate(slots):
                    ghid[side, rows_of(slot), a:b] = value[i * 128 : (i + 1) * 128]

    def project(slots, weight, out):
        given = jnp.concatenate([n2[slot] for slot in slots], axis=0)
        for side in range(2):
            for a, b in TILES:
                value = nt(given, side_by_side(weight, (side,), slice(a, b), range(16)))
                for i, slot in enumerate(slots):
                    out[side, rows_of(slot), a:b] = value[i * 128 : (i + 1) * 128]

    def units(slots):
        for slot in slots:
            rows = rows_of(slot)
            for side in range(2):
                g, u = gate[side, rows], up[side, rows]
                gh = ghid[side, rows].astype(F32)
                sig = 1.0 / (1.0 + jnp.exp(-g))
                act = g * sig
                hid[side, rows] = (act * u).astype(BF16)
                gu[side, rows] = (gh * act).astype(BF16)
                gg[side, rows] = (gh * u * (sig + act * (1.0 - sig))).astype(BF16)

    grad_parts = parts.at[pl.ds(0, 4)]

    def back(slots):
        rows = [rows_of(slot) for slot in slots]
        given = [
            (jnp.concatenate([ref[side, r] for r in rows], axis=0), weight, side)
            for ref, weight in ((gg, wg), (gu, wu))
            for side in range(2)
        ]
        for pair in range(8):
            total = None
            for value, weight, side in given:
                term = nn(value, side_by_side(weight, (side,), slice(0, 704), (2 * pair, 2 * pair + 1)))
                total = term if total is None else total + term
            for i, slot in enumerate(slots):
                grad_parts[slot, :, pair * 256 : (pair + 1) * 256] = total[i * 128 : (i + 1) * 128].astype(BF16)

    own, right, far, left = (gather.slot(i) for i in range(4))
    grad_hidden([0, 1, 2, 3])
    gather.relay()
    gather.own.wait()
    project([own], wg, gate)
    for i in range(4):
        wug.relay_far(i)
    gather.near()
    project([right, left], wg, gate)
    gather.far()
    project([far], wg, gate)
    wug.finish()
    project([0, 1, 2, 3], wu, up)
    sum4 = ScatterX(net, grad_parts, got4, got4_half)
    net.finish()
    units([far])
    back([far])
    sum4.start_far()
    units([right, left])
    back([right, left])
    sum4.start_near()
    units([own])
    back([own])
    sum4.relay_near()

    def down(m, carry):
        rows = pl.ds(pl.multiple_of(m * 256, 256), 256)
        for pair in range(8):
            total = None
            for side in range(2):
                term = nn(hid[side, rows], side_by_side(wd, (side,), slice(0, 704), (2 * pair, 2 * pair + 1)))
                total = term if total is None else total + term
            down_ref[pl.ds(2 * m, 2), :, pair * 256 : (pair + 1) * 256] = total.astype(BF16).reshape(2, 128, 256)
        return carry

    lax.fori_loop(0, 2, down, 0)
    stores.append(net.move(down_ref, down_hbm))
    for k, (ref, given, weight) in enumerate(((gg, n2, wg), (gu, n2, wu), (hid, cotg, wd))):
        for side in range(2):
            flipped[...] = ref[side].T
            for pair in range(8):
                some = given[:, :, pair * 256 : (pair + 1) * 256].reshape(512, 256)
                product = nn(flipped[...], some).astype(BF16)
                weight[side, 2 * pair] = product[:, 0:128]
                weight[side, 2 * pair + 1] = product[:, 128:256]
            stores.append(net.move(weight.at[side], grads_hbm.at[k, side]))
    sum4.wait()

    given = sum4.total()
    grad, normed = norm_back(middle_ref[...], given, gains[0:1])
    gmid_ref[...] = cot_ref[...].astype(F32) + grad
    ln2_ref[0:1] = jnp.sum(given * normed, axis=0, keepdims=True)
    ln2_ref[1:2] = jnp.sum(given, axis=0, keepdims=True)
    ln2_ref[2:8] = jnp.zeros((6, 2048), F32)
    for copy in stores:
        copy.wait()
    net.finish()


def norm_back(x, given, gain):
    center = x - jnp.mean(x, axis=-1, keepdims=True)
    scale = lax.rsqrt(jnp.mean(center * center, axis=-1, keepdims=True) + EPS)
    normed = center * scale
    q = given * gain
    grad = scale * (
        q - jnp.mean(q, axis=-1, keepdims=True) - normed * jnp.mean(q * normed, axis=-1, keepdims=True)
    )
    return grad, normed


def k2(x, att, wa, wg, pack_u, pack_d, cot, cotg):
    shapes = [
        ((128, 2048), F32, AN), ((128, 2048), F32, VM), ((4, 128, 2048), BF16, AN),
        ((3, 2, 16, ROWS_M, 128), BF16, AN), ((8, 2048), F32, VM),
    ]
    wide, tall = (2, 16, ROWS_M, 128), (2, 512, ROWS_M)
    return pl.pallas_call(
        k2_kernel,
        out_shape=[jax.ShapeDtypeStruct(s, d) for s, d, _ in shapes],
        in_specs=[VM, VM, AN, AN, VM, VM, VM, AN],
        out_specs=[m for _, _, m in shapes],
        scratch_shapes=[
            pltpu.VMEM((16, 256, 128), BF16),
            pltpu.VMEM((16, 16, 128), BF16),
            pltpu.VMEM((128, 2048), F32),
            pltpu.VMEM((4, 128, 2048), BF16),
            pltpu.VMEM((8, 128, 2048), BF16),
            pltpu.VMEM((3, 128, 2048), BF16),
            pltpu.VMEM((8, 64, 2048), BF16),
            pltpu.VMEM((8, 2048), F32),
            pltpu.VMEM((128, 2048), BF16),
            pltpu.VMEM((4, 128, 2048), BF16),
            pltpu.VMEM(wide, BF16),
            pltpu.VMEM(wide, BF16),
            pltpu.VMEM(wide, BF16),
            pltpu.VMEM((4, 128, 2048), BF16),
            pltpu.VMEM(tall, F32),
            pltpu.VMEM(tall, F32),
            pltpu.VMEM(tall, BF16),
            pltpu.VMEM(tall, BF16),
            pltpu.VMEM(tall, BF16),
            pltpu.VMEM(tall, BF16),
            pltpu.VMEM((2, 128, 2048), BF16),
            pltpu.VMEM((2, 64, 2048), BF16),
            pltpu.VMEM((ROWS_M, 512), BF16),
            pltpu.SemaphoreType.DMA((160,)),
            pltpu.SemaphoreType.DMA((160,)),
            pltpu.SemaphoreType.DMA((16,)),
        ],
        compiler_params=pltpu.CompilerParams(
            collective_id=2, has_side_effects=True, vmem_limit_bytes=62 * MIB
        ),
        name="project_norm_feed_forward",
    )(x, att, wa, wg, pack_u, pack_d, cot, cotg)


def tn(a, b):
    return lax.dot_general(a, b, (((0,), (0,)), ((), ())), preferred_element_type=F32)


class ScatterW:
    def __init__(self, net, rows, own, theirs, far, near):
        self.net, self.rows, self.half = net, rows, rows // 2
        self.own, self.theirs, self.far, self.near = own, theirs, far, near
        self.y = net.f // 4

    def at(self, step):
        return lax.rem(self.y + step, 4)

    def add(self, target, rows, *arrived):
        if len(arrived) == 1:
            target[:, rows] = target[:, rows] + arrived[0]
            return
        total = target[:, rows].astype(F32)
        for value in arrived:
            total = total + value.astype(F32)
        target[:, rows] = total.astype(BF16)

    def step_a(self):
        net, h, rows = self.net, self.half, self.rows
        lo, hi = pl.ds(0, h), pl.ds(h, rows - h)
        own, y = self.own, self.at

        def add(step):
            ref = self.theirs(y(step))
            self.add(own(y(step)), pl.ds(0, rows), ref[...])

        add(2)
        self.far_p = net.send(own(y(2)).at[:, lo], self.far.at[0], "yp")
        self.far_m = net.send(own(y(2)).at[:, hi], self.far.at[1], "ym")
        add(1)
        self.near_p = [net.send(own(y(1)).at[:, hi], self.near.at[0, :, hi], "yp")]
        add(3)
        self.near_m = [net.send(own(y(3)).at[:, lo], self.near.at[1, :, lo], "ym")]
        add(0)

    def step_b(self):
        net, h, rows = self.net, self.half, self.rows
        lo, hi = pl.ds(0, h), pl.ds(h, rows - h)
        own, y, far = self.own, self.at, self.far
        self.far_p.wait_recv()
        self.add(own(y(1)), lo, far[0])
        self.near_p.append(net.send(own(y(1)).at[:, lo], self.near.at[0, :, lo], "yp"))
        self.far_m.wait_recv()
        self.add(own(y(3)), hi, far[1])
        self.near_m.append(net.send(own(y(3)).at[:, hi], self.near.at[1, :, hi], "ym"))

    def step_c(self):
        for copy in self.near_p + self.near_m:
            copy.wait_recv()
        near = self.near
        self.add(self.own(self.y), pl.ds(0, self.rows), near[0], near[1])


def k3_kernel(
    x_ref, lens_ref, wa_hbm, gmid_ref, middle_hbm, down_hbm, ln2_ref, grads_hbm, normed_hbm, q_hbm, k_hbm, v_hbm, att_hbm,
    out_ref, dtok_ref, dm_ref, da_ref, small_ref, theirs_hbm,
    q_ref, k_ref, v_ref, att_ref, wa, gb, parts, got8, got8_half, got4, got4_half, g_own, gains, ga, dk, dv, gproj, flipped, begin_ref, cos_ref, sin_ref,
    sums, stage, far_m, near_m, by_z, theirs_a, far_a, near_a, by_z_a, small_out, small_in, small_tp, small_got,
    send_sems, recv_sems, local_sems,
):
    net = Net(send_sems, recv_sems, local_sems)
    f, t = net.f, net.t
    core, zh, y = lax.rem(f, 2), lax.rem(f // 2, 2), f // 4
    across_f = [(lax.rem(f + i, 16), t) for i in range(1, 16)]
    across_t = [(f, lax.rem(t + j, 8)) for j in range(1, 8)]
    net.greet(across_f + across_t + ["zo"])
    load_wa = net.move(wa_hbm, wa)
    units = [(k, flip) for k in range(3) for flip in (1, 0)]
    sides = (net.zl, 1 - net.zl)
    to_core, load_sums = [], []
    for u, (k, flip) in enumerate(units):
        there = stage.at[u] if u < 2 else theirs_hbm.at[u]
        to_core.append(net.send(grads_hbm.at[k, sides[flip], :, :, 1 - core], there, "c"))
        load_sums.append(net.move(grads_hbm.at[k, sides[flip], :, :, core], sums.at[u]))
    down = parts.at[pl.ds(net.zl * 4, 4)]
    load_down = net.move(down_hbm, down)
    load_rest = [net.move(q_hbm, q_ref), net.move(k_hbm, k_ref), net.move(v_hbm, v_ref), net.move(att_hbm, att_ref)]
    load_middle = net.move(middle_hbm, dtok_ref)

    def cast(i, carry):
        rows = pl.ds(pl.multiple_of(i * 32, 32), 32)
        g_own[rows] = gmid_ref[rows].astype(BF16)
        return carry

    lax.fori_loop(0, 4, cast, 0)
    gather = GatherTp(net, g_own, gb)
    gather.start()
    gather.start_z()
    position_tables(lens_ref, begin_ref, cos_ref, sin_ref)
    load_wa.wait()
    for i in range(16):
        small = wa[i // 4, i // 2 % 2, i % 2, 0:16].astype(F32)
        gains[0:2, i * 128 : (i + 1) * 128] = small[0:2]

    def unit(u):
        return ScatterW(
            net, ROWS_M, lambda yy: sums.at[u, yy], lambda yy: stage.at[u % 2, yy], far_m.at[u], near_m.at[u]
        )

    scatter = [unit(u) for u in range(6)]
    z_copies = [[] for _ in range(3)]

    staged = []

    def bring(u):
        to_core[u].wait_recv()
        staged.append(net.move(theirs_hbm.at[u], stage.at[u % 2]))

    def step_a(u):
        if u < 2:
            to_core[u].wait_recv()
        else:
            staged[u - 2].wait()
        load_sums[u].wait()
        scatter[u].step_a()
        if u < 4:
            bring(u + 2)

    def step_b(u):
        scatter[u].step_b()

    def step_c(u):
        k, flip = units[u]
        scatter[u].step_c()
        if flip:
            z_copies[k].append(net.send(sums.at[u, y, zh], by_z.at[k, 1], "zl"))
            z_copies[k].append(net.send(sums.at[u, y, 1 - zh], by_z.at[k, 2], "zo"))
        else:
            z_copies[k].append(net.send(sums.at[u, y, 1 - zh], by_z.at[k, 0], "zh"))

    def step_d(k):
        for copy in z_copies[k]:
            copy.wait_recv()

        total = sums[2 * k + 1, y, zh].astype(F32)
        for j in range(3):
            total = total + by_z[k, j].astype(F32)
        dm_ref[k] = total

    def attended_back(side):
        given = gb[pl.ds(side * 4, 4)].reshape(512, 2048)
        weight = jnp.concatenate([wa[i // 4, i // 2 % 2, i % 2, 784:1040] for i in range(16)], axis=1)
        value = nt(given, weight).astype(BF16)
        for i in range(4):
            ga[pl.ds(pl.multiple_of((2 * i + side) * 128, 128), 128)] = value[i * 128 : (i + 1) * 128]

    step_a(0)
    step_a(1)
    gather.relay()
    gather.relay_z()
    step_a(2)
    step_b(0)
    gather.relay_far()
    gather.plane()
    attended_back(net.zl)
    step_a(3)
    step_b(1)
    gather.rest()
    attended_back(1 - net.zl)
    load_down.wait()
    sum4 = ScatterX(net, down, got4, got4_half)
    sum4.start_far()
    sum4.start_near()
    for copy in load_rest:
        copy.wait()
    dk[...] = jnp.zeros_like(dk)
    dv[...] = jnp.zeros_like(dv)

    def attention_back(block):
        first, stop = block * 256, (block + 1) * 256
        q_block = q_ref[first:stop] * jnp.asarray(SCALE, BF16)
        ga_block = ga[first:stop]
        begin = begin_ref[first:stop, 0:1]
        dq = jnp.zeros((256, 256), F32)
        many_q, many_g, many_p, many_s = [], [], [], []
        for h in range(4):
            mask = head_mask(h)
            g_head = jnp.where(mask, ga_block, jnp.zeros_like(ga_block))
            scores = scores_of(q_block, k_ref[0:stop], begin, first, h)
            weights = jnp.exp(scores - jnp.max(scores, axis=-1, keepdims=True))
            probs = weights * (1.0 / jnp.sum(weights, axis=-1, keepdims=True))
            g_probs = nt(g_head, v_ref[0:stop])
            inner = jnp.sum(probs * g_probs, axis=-1, keepdims=True)
            g_scores = (probs * (g_probs - inner)).astype(BF16)
            dq = jnp.where(mask, nn(g_scores, k_ref[0:stop]), dq)
            many_q.append(jnp.where(mask, q_block, jnp.zeros_like(q_block)))
            many_g.append(g_head)
            many_p.append(probs.astype(BF16))
            many_s.append(g_scores)
        dk[0:stop] += tn(jnp.concatenate(many_s, axis=0), jnp.concatenate(many_q, axis=0))
        dv[0:stop] += tn(jnp.concatenate(many_p, axis=0), jnp.concatenate(many_g, axis=0))
        dq = turn(dq * SCALE, cos_ref[first:stop], sin_ref[first:stop], -1.0)
        gproj[first:stop, 0:256] = dq.astype(BF16)

    step_c(0)
    attention_back(0)
    attention_back(1)
    step_a(4)
    step_b(2)
    step_c(1)
    attention_back(2)
    attention_back(3)
    sum4.relay_near()
    step_a(5)

    def project_back(i, total):
        rows = pl.ds(pl.multiple_of(i * 128, 128), 128)
        d_key = turn(dk[rows], cos_ref[rows], sin_ref[rows], -1.0).astype(BF16)
        d_value = dv[rows].astype(BF16)
        gproj[rows, 256:512] = d_key
        gproj[rows, 512:768] = d_value
        row = [gproj[rows, 0:256].astype(F32), d_key.astype(F32), d_value.astype(F32)]
        return total + jnp.sum(jnp.concatenate(row, axis=1), axis=0, keepdims=True)

    bias = lax.fori_loop(0, 8, project_back, jnp.zeros((1, 768), F32))

    def normed_back(side):
        rows = [gproj[pl.ds(pl.multiple_of((2 * i + side) * 128, 128), 128)] for i in range(4)]
        rows = jnp.concatenate(rows, axis=0)
        for pair in range(8):
            weight = jnp.concatenate([wa[pair // 2, pair % 2, 0, 16:784], wa[pair // 2, pair % 2, 1, 16:784]], axis=1)
            part = nn(rows, weight).astype(BF16).reshape(4, 128, 256)
            parts[pl.ds(side * 4, 4), :, pair * 256 : (pair + 1) * 256] = part

    sum8 = ScatterTp(net, parts, got8, got8_half)
    normed_back(1 - net.zl)
    sum8.start_side()
    sum4.wait()
    load_middle.wait()
    out_ref[...] = (dtok_ref[...] + sum4.total()).astype(BF16)
    net.settle([sum4.half_p, sum4.half_m] + sum4.near_p + sum4.near_m)
    normed_back(net.zl)
    sum8.start_plane()
    step_b(3)
    step_c(2)
    for slot in range(8):
        chunk = slot % 4 * 2 + slot // 4
        flipped[0:256, slot * 128 : (slot + 1) * 128] = att_ref[chunk * 128 : (chunk + 1) * 128].T
    for pair in range(8):
        some = gb[:, :, pair * 256 : (pair + 1) * 256].reshape(1024, 256)
        product = nn(flipped[0:256], some).astype(BF16)
        wa[pair // 2, pair % 2, 0, 784:1040] = product[:, 0:128]
        wa[pair // 2, pair % 2, 1, 784:1040] = product[:, 128:256]
    net.settle([gather.zb_p, gather.zb_m, gather.fwd_p, gather.fwd_m, gather.za_p, gather.za_m, gather.fz_p, gather.fz_m])
    load_normed = net.move(normed_hbm, gb)
    sum8.relay_side()
    flipped[...] = gproj[...].T
    load_normed.wait()
    for pair in range(8):
        some = gb[:, :, pair * 256 : (pair + 1) * 256].reshape(1024, 256)
        product = nn(flipped[...], some).astype(BF16)
        wa[pair // 2, pair % 2, 0, 16:784] = product[:, 0:128]
        wa[pair // 2, pair % 2, 1, 16:784] = product[:, 128:256]
    first_core = net.send(wa.at[:, :, 1 - core, pl.ds(16, 1024)], theirs_a, "c")
    scatter_q = ScatterW(
        net, 1024, lambda yy: wa.at[yy, :, core, pl.ds(16, 1024)], lambda yy: theirs_a.at[yy], far_a, near_a
    )
    sum8.relay_across()
    step_b(4)
    step_c(3)
    first_core.wait_recv()
    scatter_q.step_a()
    sum8.relay_near()
    step_b(5)
    step_c(4)
    step_d(0)
    sum8.wait()
    given = sum8.total()
    grad, normed = norm_back(x_ref[...].astype(F32), given, gains[0:1])
    dtok_ref[...] = gmid_ref[...] + grad
    gain_sum = jnp.sum(given * normed, axis=0, keepdims=True)
    bias_sum = jnp.sum(given, axis=0, keepdims=True)
    bias_rows = jnp.concatenate([bias[:, i * 128 : (i + 1) * 128] for i in range(6)], axis=0)
    small_out[:, 4:10] = jnp.broadcast_to(bias_rows[None], (16, 6, 128))
    small_out[:, 10:16] = jnp.zeros((16, 6, 128), F32)
    for i in range(16):
        lanes = slice(i * 128, (i + 1) * 128)
        small_out[i, 0:1] = gain_sum[:, lanes]
        small_out[i, 1:2] = bias_sum[:, lanes]
        small_out[i, 2:4] = ln2_ref[0:2, lanes]
    copies = [
        net.send(small_out.at[place[0]], small_in.at[i], place) for i, place in enumerate(across_f)
    ]
    scatter_q.step_b()
    step_c(5)
    step_d(1)
    scatter_q.step_c()
    z_q = net.send(wa.at[y, 1 - zh, core, pl.ds(16, 1024)], by_z_a, "zh")
    step_d(2)
    total = small_out[f]
    for i, copy in enumerate(copies):
        copy.wait_recv()
        total = total + small_in[i]
    small_tp[...] = total
    copies = [net.send(small_tp.at[pl.ds(0, 8)], small_got.at[j], place) for j, place in enumerate(across_t)]
    z_q.wait_recv()

    da_ref[...] = wa[y, zh, core, pl.ds(16, 1024)].astype(F32) + by_z_a[...].astype(F32)
    row_id = lax.broadcasted_iota(jnp.int32, (8, 128), 0)
    total = small_tp[0:8]
    for j, copy in enumerate(copies):
        copy.wait_recv()
        total = total + jnp.where(row_id < 4, small_got[j], 0.0)
    small_ref[0:8] = total
    small_ref[8:16] = small_tp[8:16]
    net.finish()


def k3(x, lens, wa, gmid, middle, down, ln2, grads, normed, q, k, v, att):
    shapes = [
        ((128, 2048), BF16, VM), ((128, 2048), F32, VM), ((3, ROWS_M, 128), F32, VM), ((1024, 128), F32, VM),
        ((16, 128), F32, VM), ((6, 4, 2, ROWS_M, 128), BF16, AN),
    ]
    scratch = [
        ((1024, 256), BF16), ((1024, 256), BF16), ((1024, 256), BF16), ((1024, 256), BF16),
        ((4, 2, 2, ROWS_A, 128), BF16), ((8, 128, 2048), BF16), ((8, 128, 2048), BF16), ((3, 128, 2048), BF16),
        ((8, 64, 2048), BF16), ((2, 128, 2048), BF16), ((2, 64, 2048), BF16),
        ((128, 2048), BF16), ((8, 2048), F32), ((1024, 256), BF16), ((1024, 256), F32), ((1024, 256), F32),
        ((1024, 768), BF16), ((768, 1024), BF16), ((1024, 128), jnp.int32), ((1024, 128), F32), ((1024, 128), F32),
        ((6, 4, 2, ROWS_M, 128), BF16), ((2, 4, 2, ROWS_M, 128), BF16), ((6, 2, 2, ROWS_M // 2, 128), BF16),
        ((6, 2, 2, ROWS_M, 128), BF16), ((3, 3, ROWS_M, 128), BF16), ((4, 2, 1024, 128), BF16),
        ((2, 2, 512, 128), BF16), ((2, 2, 1024, 128), BF16),
        ((1024, 128), BF16), ((16, 16, 128), F32), ((15, 16, 128), F32), ((16, 128), F32), ((7, 8, 128), F32),
    ]
    return pl.pallas_call(
        k3_kernel,
        out_shape=[jax.ShapeDtypeStruct(s, d) for s, d, _ in shapes],
        in_specs=[VM, SM, AN, VM, AN, AN, VM, AN, AN, AN, AN, AN, AN],
        out_specs=[m for _, _, m in shapes],
        scratch_shapes=[pltpu.VMEM(s, d) for s, d in scratch]
        + [pltpu.SemaphoreType.DMA((160,)), pltpu.SemaphoreType.DMA((160,)), pltpu.SemaphoreType.DMA((24,))],
        compiler_params=pltpu.CompilerParams(
            collective_id=3, has_side_effects=True, vmem_limit_bytes=62 * MIB
        ),
        name="attend_back_sum_gradients",
    )(
        x, lens, wa.reshape(4, 2, 2, ROWS_A, 128), gmid, middle, down, ln2,
        grads.reshape(3, 2, 4, 2, 2, ROWS_M, 128), normed, q, k, v, att,
    )


def finish_kernel(
    out_in, dtok_in, dm_in, da_in, small_in,
    out_ref, dtok_ref, gain1, bias1, dqkv, dout, gain2, bias2, dgate, dup, ddown,
):
    out_ref[...] = out_in[...]
    dtok_ref[...] = dtok_in[...]
    for i, ref in enumerate((gain1, bias1, gain2, bias2)):
        ref[...] = small_in[i : i + 1]
    for j in range(3):
        for part in range(2):
            lanes = slice(part * 128, (part + 1) * 128)
            dqkv[j, :, lanes] = da_in[j * 256 + part * 128 : j * 256 + (part + 1) * 128].T
    dout[...] = da_in[768:1024]
    dgate[...] = dm_in[0]
    dup[...] = dm_in[1]
    ddown[...] = dm_in[2]


def finish(out, d_tokens, dm, da, small):
    shapes = [
        ((128, 2048), BF16), ((128, 2048), F32), ((1, 128), F32), ((1, 128), F32), ((3, 128, 256), F32), ((256, 128), F32),
        ((1, 128), F32), ((1, 128), F32), ((ROWS_M, 128), F32), ((ROWS_M, 128), F32), ((ROWS_M, 128), F32),
    ]
    return pl.pallas_call(
        finish_kernel,
        out_shape=[jax.ShapeDtypeStruct(s, d) for s, d in shapes],
        in_specs=[VM] * 5,
        out_specs=[VM] * 11,
        compiler_params=pltpu.CompilerParams(vmem_limit_bytes=62 * MIB),
        name="lay_out_gradients",
    )(out, d_tokens, dm, da, small)


def local(
    tokens, seq_lens, ln1_gain, ln1_bias, w_qkv, b_qkv, w_out, ln2_gain, ln2_bias, w_gate, w_up, w_down, cotangent
):
    small = small_rows(ln1_gain, ln1_bias, b_qkv, ln2_gain, ln2_bias)
    normed, wa, wg, cotg, q, k, v, att = k1(
        tokens, seq_lens, small, jnp.transpose(w_qkv, (1, 0, 2)), w_out, w_gate.T, cotangent
    )
    middle, gmid, down, grads, ln2 = k2(tokens, att, wa, wg, w_up.T, w_down, cotangent, cotg)
    out, d_tokens, dm, da, small, _ = k3(
        tokens, seq_lens, wa, gmid, middle, down, ln2, grads, normed, q, k, v, att
    )
    d_bias = lax.dynamic_slice_in_dim(
        small[4:10].reshape(3, 4, HEAD_DIM), lax.axis_index("fsdp") * 4, 4, axis=2
    )
    out, d_tokens, gain1, bias1, dqkv, dout, gain2, bias2, dgate, dup, ddown = finish(out, d_tokens, dm, da, small)
    return (
        out, d_tokens, gain1[0], bias1[0], jnp.transpose(dqkv, (1, 0, 2)), d_bias, dout, gain2[0], bias2[0], dgate.T, dup.T, ddown,
    )


def solution(mesh):
    placed = (
        P(("fsdp", "tp"), None),
        P("fsdp", None),
        P("fsdp"),
        P("fsdp"),
        P("fsdp", None, "tp"),
        P(None, "tp", "fsdp"),
        P("tp", "fsdp"),
        P("fsdp"),
        P("fsdp"),
        P("fsdp", "tp"),
        P("fsdp", "tp"),
        P("tp", "fsdp"),
        P(("fsdp", "tp"), None),
    )
    return jax.shard_map(
        local,
        mesh=mesh,
        in_specs=placed,
        out_specs=(
            P(("fsdp", "tp"), None),
            P(("fsdp", "tp"), None),
            P("fsdp"),
            P("fsdp"),
            P("fsdp", None, "tp"),
            P(None, "tp", "fsdp"),
            P("tp", "fsdp"),
            P("fsdp"),
            P("fsdp"),
            P("fsdp", "tp"),
            P("fsdp", "tp"),
            P("tp", "fsdp"),
        ),
        check_vma=False,
    )
```

```python
import math

import jax
import jax.numpy as jnp
import numpy as np
from jax import lax
from jax.experimental import pallas as pl
from jax.experimental.pallas import tpu as pltpu
from jax.sharding import PartitionSpec as P

F32 = jnp.float32
BF16 = jnp.bfloat16
HEAD_DIM = 64
ROT = 16
EPS = 1e-05
ROPE_BASE = 10000.0
MASKED = -1e30
SCALE = HEAD_DIM**-0.5
ROWS_A = 1040
ROWS_Q = 784
ROWS_M = 704
MIB = 2**20


def nt(a, b):
    return lax.dot_general(a, b, (((1,), (1,)), ((), ())), preferred_element_type=F32)


def nn(a, b):
    return lax.dot_general(a, b, (((1,), (0,)), ((), ())), preferred_element_type=F32)


class Net:
    def __init__(self, send_sems, recv_sems, local_sems):
        f, t = lax.axis_index("fsdp"), lax.axis_index("tp")
        self.f, self.t = f, t
        self.x, self.zl = t // 2, lax.rem(t, 2)
        self.send_sems, self.recv_sems, self.local_sems = send_sems, recv_sems, local_sems
        self.started, self.pending, self.locals = 0, [], 0

    def tx(self, step, flip=0):
        zl = 1 - self.zl if flip else self.zl
        return lax.rem(self.x + step, 4) * 2 + zl

    def fy(self, f, step):
        return lax.rem(f + 4 * step, 16)

    def peer(self, name):
        if not isinstance(name, str):
            return name
        f, t = self.f, self.t
        core = f + 1 - 2 * lax.rem(f, 2)
        high = f + 2 - 4 * lax.rem(f // 2, 2)
        return {
            "xp": (f, self.tx(1)),
            "xm": (f, self.tx(3)),
            "zl": (f, self.tx(0, 1)),
            "zh": (high, t),
            "zo": (high, self.tx(0, 1)),
            "yp": (self.fy(f, 1), t),
            "ym": (self.fy(f, 3), t),
            "c": (core, t),
        }[name]

    def greet(self, names):
        barrier = pltpu.get_barrier_semaphore()
        for name in names:
            pl.semaphore_signal(
                barrier, inc=1, device_id=self.peer(name), device_id_type=pl.DeviceIdType.MESH
            )
        pl.semaphore_wait(barrier, len(names))

    def send(self, src, dst, name):
        k = self.started
        copy = pltpu.make_async_remote_copy(
            src_ref=src,
            dst_ref=dst,
            send_sem=self.send_sems.at[k],
            recv_sem=self.recv_sems.at[k],
            device_id=self.peer(name),
            device_id_type=pl.DeviceIdType.MESH,
        )
        copy.start()
        self.started += 1
        self.pending.append(copy)
        return copy

    def move(self, src, dst):
        copy = pltpu.make_async_copy(src, dst, self.local_sems.at[self.locals])
        copy.start()
        self.locals += 1
        return copy

    def settle(self, copies):
        for copy in copies:
            copy.wait_send()
        done = {id(copy) for copy in copies}
        self.pending = [copy for copy in self.pending if id(copy) not in done]

    def finish(self):
        for copy in self.pending:
            copy.wait_send()
        self.pending = []


class GatherTp:
    def __init__(self, net, src, buf):
        self.net, self.buf, self.src = net, buf, src
        half = src.shape[0] // 2
        self.lo, self.hi = pl.ds(0, half), pl.ds(half, half)

    def slot(self, step, flip=0):
        zl = 1 - self.net.zl if flip else self.net.zl
        return zl * 4 + lax.rem(self.net.x + step, 4)

    def pass_on(self, slot, rows, name):
        return self.net.send(self.buf.at[slot, rows], self.buf.at[slot, rows], name)

    def start(self):
        net, lo, hi = self.net, self.lo, self.hi
        own = self.slot(0)
        self.own = net.move(self.src, self.buf.at[own])
        self.xp_lo = net.send(self.src.at[lo], self.buf.at[own, lo], "xp")
        self.xm_hi = net.send(self.src.at[hi], self.buf.at[own, hi], "xm")
        self.xp_hi = net.send(self.src.at[hi], self.buf.at[own, hi], "xp")
        self.xm_lo = net.send(self.src.at[lo], self.buf.at[own, lo], "xm")

    def start_z(self):
        self.z = self.net.send(self.src, self.buf.at[self.slot(0)], "zl")

    def relay(self):
        lo, hi = self.lo, self.hi
        left, right = self.slot(3), self.slot(1)
        self.xp_lo.wait_recv()
        self.fwd_p = self.pass_on(left, lo, "xp")
        self.xm_hi.wait_recv()
        self.fwd_m = self.pass_on(right, hi, "xm")
        self.xp_hi.wait_recv()
        self.za_p = self.pass_on(left, hi, "zl")
        self.xm_lo.wait_recv()
        self.za_m = self.pass_on(right, lo, "zl")

    def relay_z(self):
        across = self.slot(0, 1)
        self.z.wait_recv()
        self.zb_p = self.pass_on(across, self.lo, "xp")
        self.zb_m = self.pass_on(across, self.hi, "xm")

    def relay_far(self):
        self.zb_p.wait_recv()
        self.fz_p = self.pass_on(self.slot(3, 1), self.lo, "xp")
        self.zb_m.wait_recv()
        self.fz_m = self.pass_on(self.slot(1, 1), self.hi, "xm")

    def plane(self):
        self.fwd_p.wait_recv()
        self.fwd_m.wait_recv()
        self.own.wait()

    def rest(self):
        for copy in (self.za_p, self.za_m, self.fz_p, self.fz_m):
            copy.wait_recv()


class GatherX:
    def __init__(self, net, src, buf):
        self.net, self.buf, self.src = net, buf, src
        self.half = src.shape[0] // 2

    def slot(self, step):
        return lax.rem(self.net.x + step, 4)

    def start(self):
        net, h = self.net, self.half
        lo, hi = pl.ds(0, h), pl.ds(h, h)
        own = self.slot(0)
        self.own = net.move(self.src, self.buf.at[own])
        self.xp_lo = net.send(self.src.at[lo], self.buf.at[own, lo], "xp")
        self.xm_hi = net.send(self.src.at[hi], self.buf.at[own, hi], "xm")
        self.xp_hi = net.send(self.src.at[hi], self.buf.at[own, hi], "xp")
        self.xm_lo = net.send(self.src.at[lo], self.buf.at[own, lo], "xm")

    def relay(self):
        net, h = self.net, self.half
        lo, hi = pl.ds(0, h), pl.ds(h, h)
        left, right = self.slot(3), self.slot(1)
        self.xp_lo.wait_recv()
        self.fwd_p = net.send(self.buf.at[left, lo], self.buf.at[left, lo], "xp")
        self.xm_hi.wait_recv()
        self.fwd_m = net.send(self.buf.at[right, hi], self.buf.at[right, hi], "xm")

    def near(self):
        self.xp_hi.wait_recv()
        self.xm_lo.wait_recv()

    def far(self):
        self.fwd_p.wait_recv()
        self.fwd_m.wait_recv()


class GatherW:
    def __init__(self, net, src, buf, wide, offset=0):
        self.net, self.src, self.buf, self.wide, self.offset = net, src, buf, wide, offset
        self.half = src.shape[0] // 32 * 16
        f = net.f
        high = f + 2 - 4 * lax.rem(f // 2, 2)
        self.sources = [((0, f), None), ((0, high), "zh")]
        if wide:
            self.sources += [((1, f), "zl"), ((1, high), "zo")]

    def at(self, key, step, rows=None):
        flip, f = key
        f = self.net.fy(f, step)
        start, size = (0, self.src.shape[0]) if rows is None else rows
        rows = pl.ds(self.offset + start, size)
        if self.wide:
            side = 1 - self.net.zl if flip else self.net.zl
            place = (f,) if len(self.buf.shape) == 4 else (f // 4, lax.rem(f // 2, 2), lax.rem(f, 2))
            return self.buf.at[(side, *place, rows)]
        return self.buf.at[f, rows]

    def pass_on(self, key, step, name, rows=None, src=None):
        here = self.at(key, step, rows)
        return self.net.send(here if src is None else src, here, name)

    def start(self):
        net, src = self.net, self.src
        own = (0, net.f)
        self.own = net.move(src, self.at(own, 0))
        self.by_z = [
            self.pass_on(own, 0, name, src=src) for _, name in self.sources if name is not None
        ]
        self.by_y = [(self.pass_on(own, 0, "yp", src=src), self.pass_on(own, 0, "ym", src=src))]
        self.by_c = [self.pass_on(own, 0, "c", src=src)]
        self.by_y2 = []

    def relay_z(self):
        for copy, (key, _) in zip(self.by_z, self.sources[1:]):
            copy.wait_recv()
            self.by_y.append((self.pass_on(key, 0, "yp"), self.pass_on(key, 0, "ym")))
            self.by_c.append(self.pass_on(key, 0, "c"))

    def relay_y(self, i):
        key, h = self.sources[i][0], self.half
        up, down = self.by_y[i]
        rows = self.src.shape[0]
        up.wait_recv()
        fwd_up = self.pass_on(key, 3, "yp", (0, h))
        down.wait_recv()
        fwd_down = self.pass_on(key, 1, "ym", (h, rows - h))
        self.by_c.append(self.pass_on(key, 3, "c"))
        self.by_c.append(self.pass_on(key, 1, "c"))
        self.by_y2.append((fwd_up, fwd_down))

    def relay_far(self, i):
        for copy in self.by_y2[i]:
            copy.wait_recv()
        self.by_c.append(self.pass_on(self.sources[i][0], 2, "c"))

    def finish(self):
        self.own.wait()
        for copy in self.by_c:
            copy.wait_recv()


def norm_rows(x, gain, bias):
    center = x - jnp.mean(x, axis=-1, keepdims=True)
    spread = jnp.mean(center * center, axis=-1, keepdims=True)
    return center * lax.rsqrt(spread + EPS) * gain + bias


def position_tables(lens_ref, begin_ref, cos_ref, sin_ref):
    rows = begin_ref.shape[0]
    slot = lax.broadcasted_iota(jnp.int32, (rows, 128), 0)
    begin = jnp.zeros((rows, 128), jnp.int32)
    end = jnp.int32(0)
    for i in range(lens_ref.shape[1]):
        length = lens_ref[0, i]
        end = end + length
        begin = begin + jnp.where(slot >= end, length, 0)
    begin_ref[...] = begin
    lane = lax.rem(lax.broadcasted_iota(jnp.int32, (1, 128), 1), HEAD_DIM)
    which = lax.rem(lane, ROT // 2)
    frequency = jnp.zeros((1, 128), F32)
    for j in range(ROT // 2):
        value = float(np.exp(np.float32(j) * np.float32(-2.0 * math.log(ROPE_BASE) / ROT)))
        frequency = jnp.where(which == j, value, frequency)
    angle = (slot - begin).astype(F32) * frequency
    turns = jnp.floor(angle * (2.0 / math.pi) + 0.5)
    r = angle - turns * 1.5703125 - turns * 4.837512969970703125e-4 - turns * 7.54978995489188216e-8
    z = r * r
    sine = ((-1.9515295891e-4 * z + 8.3321608736e-3) * z - 1.6666654611e-1) * z * r + r
    cosine = (
        ((2.443315711809948e-5 * z - 1.388731625493765e-3) * z + 4.166664568298827e-2) * z * z
        - 0.5 * z
        + 1.0
    )
    quadrant = turns - 4.0 * jnp.floor(turns * 0.25)
    odd = (quadrant == 1.0) | (quadrant == 3.0)
    cos_all = jnp.where(odd, sine, cosine)
    cos_all = jnp.where((quadrant == 1.0) | (quadrant == 2.0), -cos_all, cos_all)
    sin_all = jnp.where(odd, cosine, sine)
    sin_all = jnp.where(quadrant >= 2.0, -sin_all, sin_all)
    cos_ref[...] = jnp.where(lane < ROT, cos_all, 1.0)
    sin_ref[...] = jnp.where(lane < ROT, sin_all, 0.0)


def turn(values, cos, sin, direction):
    lane = lax.rem(lax.broadcasted_iota(jnp.int32, (1, 256), 1), HEAD_DIM)
    cos = jnp.concatenate([cos, cos], axis=1)
    sin = jnp.concatenate([sin, sin], axis=1) * direction
    after = pltpu.roll(values, 256 - ROT // 2, 1)
    before = pltpu.roll(values, ROT // 2, 1)
    other = jnp.where(lane < ROT // 2, -after, before)
    return values * cos + other * sin


def head_mask(h):
    return lax.broadcasted_iota(jnp.int32, (1, 256), 1) // HEAD_DIM == h


def scores_of(q_block, keys, begin, first, h):
    rows, stop = q_block.shape[0], keys.shape[0]
    q_head = jnp.where(head_mask(h), q_block, jnp.zeros_like(q_block))
    scores = nt(q_head, keys)
    key_slot = lax.broadcasted_iota(jnp.int32, (rows, stop), 1)
    query_slot = lax.broadcasted_iota(jnp.int32, (rows, stop), 0) + first
    return jnp.where((key_slot >= begin) & (key_slot <= query_slot), scores, MASKED)


def flip_into(ref, first, source):
    columns = source.shape[1]
    for begin in range(0, columns, 128):
        end = min(begin + 128, columns)
        ref[first + begin : first + end] = source[:, begin:end].T


def k1_kernel(
    x_ref, lens_ref, small_ref, w_qkv, w_out, pack_g, cot_ref,
    normed_hbm, wa_hbm, wg_hbm, cotg_hbm, q_hbm, k_hbm, v_hbm, att_hbm,
    normed_ref, wa_ref, wg_ref, cotg_ref, q_ref, k_ref, v_ref, att_ref,
    pack_a, raw, gains, biases, begin_ref, cos_ref, sin_ref, send_sems, recv_sems, local_sems,
):
    net = Net(send_sems, recv_sems, local_sems)
    pack_a[0:16] = small_ref[...]
    for j in range(3):
        flip_into(pack_a, 16 + 256 * j, w_qkv.at[j])
    net.greet(["xp", "xm", "zl", "zh", "zo", "yp", "ym", "c"])
    tokens = GatherTp(net, x_ref, raw)
    wa = GatherW(net, pack_a, wa_ref, False)
    wo = GatherW(net, w_out, wa_ref, False, ROWS_Q)
    wg = GatherW(net, pack_g, wg_ref, True)
    cot = GatherX(net, cot_ref, cotg_ref)
    wa.start()
    tokens.start()
    position_tables(lens_ref, begin_ref, cos_ref, sin_ref)
    wa.relay_z()
    tokens.start_z()
    wg.start()
    wa.relay_y(0)
    tokens.relay()
    wa.relay_far(0)
    wa.relay_y(1)
    wa.relay_far(1)
    tokens.relay_z()
    wa.finish()
    stores = []
    for f in range(16):
        small = wa_ref[f, 0:16].astype(F32)
        gains[0:2, f * 128 : (f + 1) * 128] = small[0:2]
        biases[0:16, :] = small if f == 0 else biases[0:16, :] + small

    def project(side):
        def norm_some(i, carry):
            values = raw[side * 4 + i].astype(F32)
            normed_ref[i * 2 + side] = norm_rows(values, gains[0:1, :], gains[1:2, :]).astype(BF16)
            return carry

        lax.fori_loop(0, 4, norm_some, 0)

        def some_rows(i, carry):
            chunks = [2 * (2 * i + n) + side for n in range(2)]
            given = jnp.concatenate([normed_ref[chunk] for chunk in chunks], axis=0)
            rows = [pl.ds(pl.multiple_of(chunk * 128, 128), 128) for chunk in chunks]
            cos = jnp.concatenate([cos_ref[r] for r in rows], axis=0)
            sin = jnp.concatenate([sin_ref[r] for r in rows], axis=0)
            for j, out in enumerate((q_ref, k_ref, v_ref)):
                lines = slice(16 + 256 * j, 16 + 256 * (j + 1))
                total = nt(given, jnp.concatenate([wa_ref[f, lines] for f in range(16)], axis=1))
                total = total + jnp.concatenate([biases[4 + 2 * j : 5 + 2 * j], biases[5 + 2 * j : 6 + 2 * j]], axis=1)
                if j < 2:
                    total = turn(total, cos, sin, 1.0)
                for n in range(2):
                    out[rows[n]] = total[n * 128 : (n + 1) * 128].astype(BF16)
            return carry

        lax.fori_loop(0, 2, some_rows, 0)

    tokens.plane()
    wg.relay_y(0)
    project(net.zl)
    tokens.relay_far()
    wo.start()
    wg.relay_z()
    cot.start()
    wg.relay_far(0)
    tokens.rest()
    project(1 - net.zl)
    stores += [net.move(normed_ref, normed_hbm), net.move(q_ref, q_hbm)]
    stores += [net.move(k_ref, k_hbm), net.move(v_ref, v_hbm)]
    wg.relay_y(1)
    for block in range(4):
        first, stop = block * 256, (block + 1) * 256
        q_block = q_ref[first:stop] * jnp.asarray(SCALE, BF16)
        begin = begin_ref[first:stop, 0:1]
        mixed = jnp.zeros((256, 256), F32)
        for h in range(4):
            scores = scores_of(q_block, k_ref[0:stop], begin, first, h)
            weights = jnp.exp(scores - jnp.max(scores, axis=-1, keepdims=True))
            probs = (weights * (1.0 / jnp.sum(weights, axis=-1, keepdims=True))).astype(BF16)
            mixed = jnp.where(head_mask(h), nn(probs, v_ref[0:stop]), mixed)
        att_ref[first:stop] = mixed.astype(BF16)
        if block == 1:
            wg.relay_y(2)
            wo.relay_z()
        if block == 2:
            wg.relay_y(3)
            wg.relay_far(1)
            wo.relay_y(0)
    stores.append(net.move(att_ref, att_hbm))
    cot.relay()
    wo.relay_y(1)
    wg.relay_far(2)
    wg.relay_far(3)
    wo.relay_far(0)
    wo.relay_far(1)
    wg.finish()
    stores.append(net.move(wg_ref, wg_hbm))
    wo.finish()
    stores.append(net.move(wa_ref, wa_hbm))
    cot.own.wait()
    cot.near()
    cot.far()
    stores.append(net.move(cotg_ref, cotg_hbm))
    for copy in stores:
        copy.wait()
    net.finish()


def hbm(shape, dtype=BF16):
    return jax.ShapeDtypeStruct(shape, dtype)


VM = pl.BlockSpec(memory_space=pltpu.VMEM)
SM = pl.BlockSpec(memory_space=pltpu.SMEM)
AN = pl.BlockSpec(memory_space=pl.ANY)


def k1(x, lens, small, w_qkv, w_out, pack_g, cot):
    shapes = [
        (8, 128, 2048), (16, ROWS_A, 128), (2, 16, ROWS_M, 128), (4, 128, 2048),
        (1024, 256), (1024, 256), (1024, 256), (1024, 256),
    ]
    return pl.pallas_call(
        k1_kernel,
        out_shape=[hbm(s) for s in shapes],
        in_specs=[VM, SM, VM, VM, VM, VM, VM],
        out_specs=[AN] * 8,
        scratch_shapes=[pltpu.VMEM(s, BF16) for s in shapes + [(ROWS_Q, 128)]]
        + [
            pltpu.VMEM((8, 128, 2048), BF16),
            pltpu.VMEM((8, 2048), F32),
            pltpu.VMEM((16, 128), F32),
            pltpu.VMEM((1024, 128), jnp.int32),
            pltpu.VMEM((1024, 128), F32),
            pltpu.VMEM((1024, 128), F32),
            pltpu.SemaphoreType.DMA((160,)),
            pltpu.SemaphoreType.DMA((160,)),
            pltpu.SemaphoreType.DMA((16,)),
        ],
        compiler_params=pltpu.CompilerParams(
            collective_id=1, has_side_effects=True, vmem_limit_bytes=56 * MIB
        ),
        name="gather_project_attend",
    )(x, lens, small, w_qkv, w_out, pack_g, cot)


def small_rows(ln1_gain, ln1_bias, b_qkv, ln2_gain, ln2_bias):
    spread = jnp.zeros((3, 4, 16, 4), BF16)
    spread = lax.dynamic_update_slice(
        spread, b_qkv.reshape(3, 4, 1, 4), (0, 0, lax.axis_index("fsdp"), 0)
    ).reshape(6, 128)
    rows = lax.broadcasted_iota(jnp.int32, (16, 128), 0)
    small = jnp.pad(spread, ((4, 6), (0, 0)))
    for i, row in enumerate((ln1_gain, ln1_bias, ln2_gain, ln2_bias)):
        small = jnp.where(rows == i, row[None, :], small)
    return small


class ScatterTp:
    def __init__(self, net, parts, got, got_half):
        self.net, self.parts, self.got, self.got_half = net, parts, got, got_half
        half = parts.shape[1] // 2
        self.lo, self.hi = pl.ds(0, half), pl.ds(half, half)

    slot = GatherTp.slot

    def half_to(self, slot, rows, name, place):
        return self.net.send(self.parts.at[slot, rows], self.got_half.at[place], name)

    def add(self, slot, rows, *places):
        total = self.parts[slot, rows].astype(F32)
        for place in places:
            total = total + self.got_half[place].astype(F32)
        self.parts[slot, rows] = total.astype(BF16)

    def start_side(self):
        lo, hi = self.lo, self.hi
        self.zx2 = [self.half_to(self.slot(2, 1), lo, "xm", 0), self.half_to(self.slot(2, 1), hi, "xp", 1)]
        self.by_z = [self.half_to(self.slot(3, 1), hi, "zl", 2), self.half_to(self.slot(1, 1), lo, "zl", 4)]

    def start_plane(self):
        net, parts, lo, hi = self.net, self.parts, self.lo, self.hi
        far, left, right = self.slot(2), self.slot(3), self.slot(1)
        self.x2 = [self.half_to(far, hi, "xm", 6), self.half_to(far, lo, "xp", 7)]
        self.near_m = [net.send(parts.at[left, lo], self.got.at[1, lo], "xm")]
        self.near_p = [net.send(parts.at[right, hi], self.got.at[2, hi], "xp")]

    def relay_side(self):
        lo, hi = self.lo, self.hi
        self.zx2[0].wait_recv()
        self.add(self.slot(3, 1), lo, 0)
        self.across = [self.half_to(self.slot(3, 1), lo, "xm", 3)]
        self.zx2[1].wait_recv()
        self.add(self.slot(1, 1), hi, 1)
        self.across.append(self.half_to(self.slot(1, 1), hi, "xp", 5))

    def relay_across(self):
        across = self.slot(0, 1)
        self.across[0].wait_recv()
        self.add(across, self.lo, 3)
        self.across[1].wait_recv()
        self.add(across, self.hi, 5)
        self.z_own = self.net.send(self.parts.at[across], self.got.at[0], "zl")

    def relay_near(self):
        net, parts, lo, hi = self.net, self.parts, self.lo, self.hi
        left, right = self.slot(3), self.slot(1)
        self.by_z[0].wait_recv()
        self.x2[0].wait_recv()
        self.add(left, hi, 2, 6)
        self.near_m.append(net.send(parts.at[left, hi], self.got.at[1, hi], "xm"))
        self.by_z[1].wait_recv()
        self.x2[1].wait_recv()
        self.add(right, lo, 4, 7)
        self.near_p.append(net.send(parts.at[right, lo], self.got.at[2, lo], "xp"))

    def wait(self):
        self.z_own.wait_recv()
        for copy in self.near_p + self.near_m:
            copy.wait_recv()

    def total(self):
        total = self.parts[self.slot(0)].astype(F32)
        for i in range(3):
            total = total + self.got[i].astype(F32)
        return total


class ScatterX:
    def __init__(self, net, parts, got, got_half):
        self.net, self.parts, self.got, self.got_half = net, parts, got, got_half
        self.half = parts.shape[1] // 2

    slot = GatherX.slot

    def add(self, slot, rows, arrived):
        total = self.parts[slot, rows].astype(F32) + arrived[...].astype(F32)
        self.parts[slot, rows] = total.astype(BF16)

    def start_far(self):
        net, h, parts = self.net, self.half, self.parts
        far = self.slot(2)
        self.half_p = net.send(parts.at[far, pl.ds(0, h)], self.got_half.at[0], "xp")
        self.half_m = net.send(parts.at[far, pl.ds(h, h)], self.got_half.at[1], "xm")

    def start_near(self):
        net, h, parts = self.net, self.half, self.parts
        right, left = self.slot(1), self.slot(3)
        self.near_p = [net.send(parts.at[right, pl.ds(h, h)], self.got.at[0, pl.ds(h, h)], "xp")]
        self.near_m = [net.send(parts.at[left, pl.ds(0, h)], self.got.at[1, pl.ds(0, h)], "xm")]

    def relay_near(self):
        net, h, parts = self.net, self.half, self.parts
        right, left = self.slot(1), self.slot(3)
        self.half_p.wait_recv()
        self.add(right, pl.ds(0, h), self.got_half.at[0])
        self.near_p.append(net.send(parts.at[right, pl.ds(0, h)], self.got.at[0, pl.ds(0, h)], "xp"))
        self.half_m.wait_recv()
        self.add(left, pl.ds(h, h), self.got_half.at[1])
        self.near_m.append(net.send(parts.at[left, pl.ds(h, h)], self.got.at[1, pl.ds(h, h)], "xm"))

    def wait(self):
        for copy in self.near_p + self.near_m:
            copy.wait_recv()

    def total(self):
        total = self.parts[self.slot(0)].astype(F32)
        return total + self.got[0].astype(F32) + self.got[1].astype(F32)


def side_by_side(ref, lead, lines, slabs):
    return jnp.concatenate([ref[(*lead, f, lines)] for f in slabs], axis=1)


TILES = ((0, 256), (256, 512), (512, 704))


def k2_kernel(
    x_ref, att_ref, wa_hbm, wg_hbm, pack_u, pack_d, cot_ref, cotg_hbm,
    middle_hbm, gmid_ref, down_hbm, grads_hbm, ln2_ref,
    wo, small_ref, middle_ref, down_ref, parts, got8, got8_half, gains, n2_own, n2, wg, wu, wd, cotg, gate, up, ghid, hid, gg, gu, got4, got4_half, flipped,
    send_sems, recv_sems, local_sems,
):
    net = Net(send_sems, recv_sems, local_sems)
    net.greet(["xp", "xm", "zl", "zh", "zo", "yp", "ym", "c"])
    wug = GatherW(net, pack_u, wu, True)
    wdg = GatherW(net, pack_d, wd, True)
    wdg.start()
    first = [net.move(wa_hbm.at[:, pl.ds(784, 256)], wo), net.move(wa_hbm.at[:, pl.ds(0, 16)], small_ref)]
    moves = [net.move(wg_hbm, wg), net.move(cotg_hbm, cotg)]
    for copy in first:
        copy.wait()
    sum8 = ScatterTp(net, parts, got8, got8_half)

    def attention_out(side):
        rows = [att_ref[pl.ds(pl.multiple_of((2 * i + side) * 128, 128), 128)] for i in range(4)]
        rows = jnp.concatenate(rows, axis=0)
        for pair in range(8):
            weight = side_by_side(wo, (), slice(0, 256), (2 * pair, 2 * pair + 1))
            part = nn(rows, weight).astype(BF16).reshape(4, 128, 256)
            parts[pl.ds(side * 4, 4), :, pair * 256 : (pair + 1) * 256] = part

    attention_out(1 - net.zl)
    sum8.start_side()
    attention_out(net.zl)
    for f in range(16):
        small = small_ref[f].astype(F32)
        gains[0:2, f * 128 : (f + 1) * 128] = small[2:4]
    sum8.start_plane()
    sum8.relay_side()
    wdg.relay_z()
    wug.start()
    wdg.relay_y(0)
    sum8.relay_across()
    for i in range(1, 4):
        wdg.relay_y(i)
    wug.relay_z()
    sum8.relay_near()
    for i in range(4):
        wdg.relay_far(i)
    wug.relay_y(0)
    sum8.wait()
    middle = x_ref[...].astype(F32) + sum8.total()
    middle_ref[...] = middle
    n2_own[...] = norm_rows(middle, gains[0:1], gains[1:2]).astype(BF16)
    gather = GatherX(net, n2_own, n2)
    gather.start()
    stores = [net.move(middle_ref, middle_hbm)]
    for copy in moves:
        copy.wait()
    for i in range(1, 4):
        wug.relay_y(i)
    wdg.finish()

    def rows_of(slot):
        return pl.ds(slot * 128 if isinstance(slot, int) else pl.multiple_of(slot * 128, 128), 128)

    def grad_hidden(slots):
        given = jnp.concatenate([cotg[slot] for slot in slots], axis=0)
        for side in range(2):
            for a, b in TILES:
                value = nt(given, side_by_side(wd, (side,), slice(a, b), range(16))).astype(BF16)
                for i, slot in enumerate(slots):
                    ghid[side, rows_of(slot), a:b] = value[i * 128 : (i + 1) * 128]

    def project(slots, weight, out):
        given = jnp.concatenate([n2[slot] for slot in slots], axis=0)
        for side in range(2):
            for a, b in TILES:
                value = nt(given, side_by_side(weight, (side,), slice(a, b), range(16)))
                for i, slot in enumerate(slots):
                    out[side, rows_of(slot), a:b] = value[i * 128 : (i + 1) * 128]

    def units(slots):
        for slot in slots:
            rows = rows_of(slot)
            for side in range(2):
                g, u = gate[side, rows], up[side, rows]
                gh = ghid[side, rows].astype(F32)
                sig = 1.0 / (1.0 + jnp.exp(-g))
                act = g * sig
                hid[side, rows] = (act * u).astype(BF16)
                gu[side, rows] = (gh * act).astype(BF16)
                gg[side, rows] = (gh * u * (sig + act * (1.0 - sig))).astype(BF16)

    grad_parts = parts.at[pl.ds(0, 4)]

    def back(slots):
        rows = [rows_of(slot) for slot in slots]
        given = [
            (jnp.concatenate([ref[side, r] for r in rows], axis=0), weight, side)
            for ref, weight in ((gg, wg), (gu, wu))
            for side in range(2)
        ]
        for pair in range(8):
            total = None
            for value, weight, side in given:
                term = nn(value, side_by_side(weight, (side,), slice(0, 704), (2 * pair, 2 * pair + 1)))
                total = term if total is None else total + term
            for i, slot in enumerate(slots):
                grad_parts[slot, :, pair * 256 : (pair + 1) * 256] = total[i * 128 : (i + 1) * 128].astype(BF16)

    own, right, far, left = (gather.slot(i) for i in range(4))
    grad_hidden([0, 1, 2, 3])
    gather.relay()
    gather.own.wait()
    project([own], wg, gate)
    for i in range(4):
        wug.relay_far(i)
    gather.near()
    project([right, left], wg, gate)
    gather.far()
    project([far], wg, gate)
    wug.finish()
    project([0, 1, 2, 3], wu, up)
    sum4 = ScatterX(net, grad_parts, got4, got4_half)
    net.finish()
    units([far])
    back([far])
    sum4.start_far()
    units([right, left])
    back([right, left])
    sum4.start_near()
    units([own])
    back([own])
    sum4.relay_near()

    def down(m, carry):
        rows = pl.ds(pl.multiple_of(m * 256, 256), 256)
        for pair in range(8):
            total = None
            for side in range(2):
                term = nn(hid[side, rows], side_by_side(wd, (side,), slice(0, 704), (2 * pair, 2 * pair + 1)))
                total = term if total is None else total + term
            down_ref[pl.ds(2 * m, 2), :, pair * 256 : (pair + 1) * 256] = total.astype(BF16).reshape(2, 128, 256)
        return carry

    lax.fori_loop(0, 2, down, 0)
    stores.append(net.move(down_ref, down_hbm))
    for k, (ref, given, weight) in enumerate(((gg, n2, wg), (gu, n2, wu), (hid, cotg, wd))):
        for side in range(2):
            flipped[...] = ref[side].T
            for pair in range(8):
                some = given[:, :, pair * 256 : (pair + 1) * 256].reshape(512, 256)
                product = nn(flipped[...], some).astype(BF16)
                weight[side, 2 * pair] = product[:, 0:128]
                weight[side, 2 * pair + 1] = product[:, 128:256]
            stores.append(net.move(weight.at[side], grads_hbm.at[k, side]))
    sum4.wait()

    given = sum4.total()
    grad, normed = norm_back(middle_ref[...], given, gains[0:1])
    gmid_ref[...] = cot_ref[...].astype(F32) + grad
    ln2_ref[0:1] = jnp.sum(given * normed, axis=0, keepdims=True)
    ln2_ref[1:2] = jnp.sum(given, axis=0, keepdims=True)
    ln2_ref[2:8] = jnp.zeros((6, 2048), F32)
    for copy in stores:
        copy.wait()
    net.finish()


def norm_back(x, given, gain):
    center = x - jnp.mean(x, axis=-1, keepdims=True)
    scale = lax.rsqrt(jnp.mean(center * center, axis=-1, keepdims=True) + EPS)
    normed = center * scale
    q = given * gain
    grad = scale * (
        q - jnp.mean(q, axis=-1, keepdims=True) - normed * jnp.mean(q * normed, axis=-1, keepdims=True)
    )
    return grad, normed


def k2(x, att, wa, wg, pack_u, pack_d, cot, cotg):
    shapes = [
        ((128, 2048), F32, AN), ((128, 2048), F32, VM), ((4, 128, 2048), BF16, AN),
        ((3, 2, 16, ROWS_M, 128), BF16, AN), ((8, 2048), F32, VM),
    ]
    wide, tall = (2, 16, ROWS_M, 128), (2, 512, ROWS_M)
    return pl.pallas_call(
        k2_kernel,
        out_shape=[jax.ShapeDtypeStruct(s, d) for s, d, _ in shapes],
        in_specs=[VM, VM, AN, AN, VM, VM, VM, AN],
        out_specs=[m for _, _, m in shapes],
        scratch_shapes=[
            pltpu.VMEM((16, 256, 128), BF16),
            pltpu.VMEM((16, 16, 128), BF16),
            pltpu.VMEM((128, 2048), F32),
            pltpu.VMEM((4, 128, 2048), BF16),
            pltpu.VMEM((8, 128, 2048), BF16),
            pltpu.VMEM((3, 128, 2048), BF16),
            pltpu.VMEM((8, 64, 2048), BF16),
            pltpu.VMEM((8, 2048), F32),
            pltpu.VMEM((128, 2048), BF16),
            pltpu.VMEM((4, 128, 2048), BF16),
            pltpu.VMEM(wide, BF16),
            pltpu.VMEM(wide, BF16),
            pltpu.VMEM(wide, BF16),
            pltpu.VMEM((4, 128, 2048), BF16),
            pltpu.VMEM(tall, F32),
            pltpu.VMEM(tall, F32),
            pltpu.VMEM(tall, BF16),
            pltpu.VMEM(tall, BF16),
            pltpu.VMEM(tall, BF16),
            pltpu.VMEM(tall, BF16),
            pltpu.VMEM((2, 128, 2048), BF16),
            pltpu.VMEM((2, 64, 2048), BF16),
            pltpu.VMEM((ROWS_M, 512), BF16),
            pltpu.SemaphoreType.DMA((160,)),
            pltpu.SemaphoreType.DMA((160,)),
            pltpu.SemaphoreType.DMA((16,)),
        ],
        compiler_params=pltpu.CompilerParams(
            collective_id=2, has_side_effects=True, vmem_limit_bytes=63 * MIB
        ),
        name="project_norm_feed_forward",
    )(x, att, wa, wg, pack_u, pack_d, cot, cotg)


def tn(a, b):
    return lax.dot_general(a, b, (((0,), (0,)), ((), ())), preferred_element_type=F32)


class ScatterW:
    def __init__(self, net, rows, own, theirs, far, near):
        self.net, self.rows, self.half = net, rows, rows // 2
        self.own, self.theirs, self.far, self.near = own, theirs, far, near
        self.y = net.f // 4

    def at(self, step):
        return lax.rem(self.y + step, 4)

    def add(self, target, rows, *arrived):
        if len(arrived) == 1:
            target[:, rows] = target[:, rows] + arrived[0]
            return
        total = target[:, rows].astype(F32)
        for value in arrived:
            total = total + value.astype(F32)
        target[:, rows] = total.astype(BF16)

    def step_a(self):
        net, h, rows = self.net, self.half, self.rows
        lo, hi = pl.ds(0, h), pl.ds(h, rows - h)
        own, y = self.own, self.at

        def add(step):
            ref = self.theirs(y(step))
            self.add(own(y(step)), pl.ds(0, rows), ref[...])

        add(2)
        self.far_p = net.send(own(y(2)).at[:, lo], self.far.at[0], "yp")
        self.far_m = net.send(own(y(2)).at[:, hi], self.far.at[1], "ym")
        add(1)
        self.near_p = [net.send(own(y(1)).at[:, hi], self.near.at[0, :, hi], "yp")]
        add(3)
        self.near_m = [net.send(own(y(3)).at[:, lo], self.near.at[1, :, lo], "ym")]
        add(0)

    def step_b(self):
        net, h, rows = self.net, self.half, self.rows
        lo, hi = pl.ds(0, h), pl.ds(h, rows - h)
        own, y, far = self.own, self.at, self.far
        self.far_p.wait_recv()
        self.add(own(y(1)), lo, far[0])
        self.near_p.append(net.send(own(y(1)).at[:, lo], self.near.at[0, :, lo], "yp"))
        self.far_m.wait_recv()
        self.add(own(y(3)), hi, far[1])
        self.near_m.append(net.send(own(y(3)).at[:, hi], self.near.at[1, :, hi], "ym"))

    def step_c(self):
        for copy in self.near_p + self.near_m:
            copy.wait_recv()
        near = self.near
        self.add(self.own(self.y), pl.ds(0, self.rows), near[0], near[1])


FIRST_PIECES = ((384, 1024), (0, 384))


def k3_kernel(
    x_ref, lens_ref, wa_hbm, gmid_ref, middle_hbm, down_hbm, ln2_ref, grads_hbm, normed_hbm, q_hbm, k_hbm, v_hbm, att_hbm,
    out_ref, dtok_ref, dm_ref, da_ref, small_ref, theirs_hbm,
    q_ref, k_ref, v_ref, att_ref, wa, gb, parts, got8, got8_half, got4, got4_half, g_own, gains, ga, dk, dv, gproj, flipped, begin_ref, cos_ref, sin_ref,
    sums, stage, far_m, near_m, by_z, theirs_a, far_a, near_a, by_z_a, small_out, small_in, small_tp, small_got,
    send_sems, recv_sems, local_sems,
):
    net = Net(send_sems, recv_sems, local_sems)
    f, t = net.f, net.t
    core, zh, y = lax.rem(f, 2), lax.rem(f // 2, 2), f // 4
    across_f = [(lax.rem(f + i, 16), t) for i in range(1, 16)]
    across_t = [(f, lax.rem(t + j, 8)) for j in range(1, 8)]
    net.greet(across_f + across_t + ["zo"])
    load_wa = net.move(wa_hbm, wa)
    units = [(k, flip) for k in range(3) for flip in (1, 0)]
    sides = (net.zl, 1 - net.zl)
    to_core, load_sums = [], []
    for u, (k, flip) in enumerate(units):
        there = stage.at[u] if u < 2 else theirs_hbm.at[u]
        to_core.append(net.send(grads_hbm.at[k, sides[flip], :, :, 1 - core], there, "c"))
        load_sums.append(net.move(grads_hbm.at[k, sides[flip], :, :, core], sums.at[u]))
    down = parts.at[pl.ds(net.zl * 4, 4)]
    load_down = net.move(down_hbm, down)
    load_rest = [net.move(q_hbm, q_ref), net.move(k_hbm, k_ref), net.move(v_hbm, v_ref), net.move(att_hbm, att_ref)]
    load_middle = net.move(middle_hbm, dtok_ref)

    def cast(i, carry):
        rows = pl.ds(pl.multiple_of(i * 32, 32), 32)
        g_own[rows] = gmid_ref[rows].astype(BF16)
        return carry

    lax.fori_loop(0, 4, cast, 0)
    gather = GatherTp(net, g_own, gb)
    gather.start()
    gather.start_z()
    position_tables(lens_ref, begin_ref, cos_ref, sin_ref)
    load_wa.wait()
    for i in range(16):
        small = wa[i // 4, i // 2 % 2, i % 2, 0:16].astype(F32)
        gains[0:2, i * 128 : (i + 1) * 128] = small[0:2]

    def unit(u):
        return ScatterW(
            net, ROWS_M, lambda yy: sums.at[u, yy], lambda yy: stage.at[u % 2, yy], far_m.at[u], near_m.at[u]
        )

    scatter = [unit(u) for u in range(6)]
    z_copies = [[] for _ in range(3)]

    staged = []

    def bring(u):
        to_core[u].wait_recv()
        staged.append(net.move(theirs_hbm.at[u], stage.at[u % 2]))

    def step_a(u):
        if u < 2:
            to_core[u].wait_recv()
        else:
            staged[u - 2].wait()
        load_sums[u].wait()
        scatter[u].step_a()
        if u < 4:
            bring(u + 2)

    def step_b(u):
        scatter[u].step_b()

    def step_c(u):
        k, flip = units[u]
        scatter[u].step_c()
        if flip:
            z_copies[k].append(net.send(sums.at[u, y, zh], by_z.at[k, 1], "zl"))
            z_copies[k].append(net.send(sums.at[u, y, 1 - zh], by_z.at[k, 2], "zo"))
        else:
            z_copies[k].append(net.send(sums.at[u, y, 1 - zh], by_z.at[k, 0], "zh"))

    def step_d(k):
        for copy in z_copies[k]:
            copy.wait_recv()

        total = sums[2 * k + 1, y, zh].astype(F32)
        for j in range(3):
            total = total + by_z[k, j].astype(F32)
        dm_ref[k] = total

    def attended_back(side):
        given = gb[pl.ds(side * 4, 4)].reshape(512, 2048)
        weight = jnp.concatenate([wa[i // 4, i // 2 % 2, i % 2, 784:1040] for i in range(16)], axis=1)
        value = nt(given, weight).astype(BF16)
        for i in range(4):
            ga[pl.ds(pl.multiple_of((2 * i + side) * 128, 128), 128)] = value[i * 128 : (i + 1) * 128]

    step_a(0)
    step_a(1)
    gather.relay()
    gather.relay_z()
    step_a(2)
    step_b(0)
    gather.relay_far()
    gather.plane()
    attended_back(net.zl)
    step_a(3)
    step_b(1)
    gather.rest()
    attended_back(1 - net.zl)
    load_down.wait()
    sum4 = ScatterX(net, down, got4, got4_half)
    sum4.start_far()
    sum4.start_near()
    for copy in load_rest:
        copy.wait()
    dk[...] = jnp.zeros_like(dk)
    dv[...] = jnp.zeros_like(dv)

    def attention_back(block):
        first, stop = block * 256, (block + 1) * 256
        q_block = q_ref[first:stop] * jnp.asarray(SCALE, BF16)
        ga_block = ga[first:stop]
        begin = begin_ref[first:stop, 0:1]
        dq = jnp.zeros((256, 256), F32)
        many_q, many_g, many_p, many_s = [], [], [], []
        for h in range(4):
            mask = head_mask(h)
            g_head = jnp.where(mask, ga_block, jnp.zeros_like(ga_block))
            scores = scores_of(q_block, k_ref[0:stop], begin, first, h)
            weights = jnp.exp(scores - jnp.max(scores, axis=-1, keepdims=True))
            probs = weights * (1.0 / jnp.sum(weights, axis=-1, keepdims=True))
            g_probs = nt(g_head, v_ref[0:stop])
            inner = jnp.sum(probs * g_probs, axis=-1, keepdims=True)
            g_scores = (probs * (g_probs - inner)).astype(BF16)
            dq = jnp.where(mask, nn(g_scores, k_ref[0:stop]), dq)
            many_q.append(jnp.where(mask, q_block, jnp.zeros_like(q_block)))
            many_g.append(g_head)
            many_p.append(probs.astype(BF16))
            many_s.append(g_scores)
        dk[0:stop] += tn(jnp.concatenate(many_s, axis=0), jnp.concatenate(many_q, axis=0))
        dv[0:stop] += tn(jnp.concatenate(many_p, axis=0), jnp.concatenate(many_g, axis=0))
        dq = turn(dq * SCALE, cos_ref[first:stop], sin_ref[first:stop], -1.0)
        gproj[first:stop, 0:256] = dq.astype(BF16)

    attention_back(0)
    attention_back(1)
    attention_back(2)
    attention_back(3)
    sum4.relay_near()

    def project_back(i, total):
        rows = pl.ds(pl.multiple_of(i * 128, 128), 128)
        d_key = turn(dk[rows], cos_ref[rows], sin_ref[rows], -1.0).astype(BF16)
        d_value = dv[rows].astype(BF16)
        gproj[rows, 256:512] = d_key
        gproj[rows, 512:768] = d_value
        row = [gproj[rows, 0:256].astype(F32), d_key.astype(F32), d_value.astype(F32)]
        return total + jnp.sum(jnp.concatenate(row, axis=1), axis=0, keepdims=True)

    bias = lax.fori_loop(0, 8, project_back, jnp.zeros((1, 768), F32))

    def normed_back(side):
        rows = [gproj[pl.ds(pl.multiple_of((2 * i + side) * 128, 128), 128)] for i in range(4)]
        rows = jnp.concatenate(rows, axis=0)
        for pair in range(8):
            weight = jnp.concatenate([wa[pair // 2, pair % 2, 0, 16:784], wa[pair // 2, pair % 2, 1, 16:784]], axis=1)
            part = nn(rows, weight).astype(BF16).reshape(4, 128, 256)
            parts[pl.ds(side * 4, 4), :, pair * 256 : (pair + 1) * 256] = part

    sum8 = ScatterTp(net, parts, got8, got8_half)
    normed_back(1 - net.zl)
    sum8.start_side()
    step_a(4)
    sum4.wait()
    load_middle.wait()
    out_ref[...] = (dtok_ref[...] + sum4.total()).astype(BF16)
    net.settle([sum4.half_p, sum4.half_m] + sum4.near_p + sum4.near_m)
    normed_back(net.zl)
    sum8.start_plane()
    step_c(0)
    step_b(2)
    step_a(5)
    step_c(1)
    step_b(3)
    step_c(2)
    for slot in range(8):
        chunk = slot % 4 * 2 + slot // 4
        flipped[0:256, slot * 128 : (slot + 1) * 128] = att_ref[chunk * 128 : (chunk + 1) * 128].T
    for pair in range(8):
        some = gb[:, :, pair * 256 : (pair + 1) * 256].reshape(1024, 256)
        product = nn(flipped[0:256], some).astype(BF16)
        wa[pair // 2, pair % 2, 0, 784:1040] = product[:, 0:128]
        wa[pair // 2, pair % 2, 1, 784:1040] = product[:, 128:256]
    net.settle([gather.zb_p, gather.zb_m, gather.fwd_p, gather.fwd_m, gather.za_p, gather.za_m, gather.fz_p, gather.fz_m])
    load_normed = net.move(normed_hbm, gb)
    sum8.relay_side()
    flipped[...] = gproj[...].T
    load_normed.wait()
    for pair in range(8):
        some = gb[:, :, pair * 256 : (pair + 1) * 256].reshape(1024, 256)
        product = nn(flipped[...], some).astype(BF16)
        wa[pair // 2, pair % 2, 0, 16:784] = product[:, 0:128]
        wa[pair // 2, pair % 2, 1, 16:784] = product[:, 128:256]
    first_core = net.send(wa.at[:, :, 1 - core, pl.ds(16, 1024)], theirs_a, "c")
    scatter_q = [
        ScatterW(
            net, end - begin,
            lambda yy, begin=begin, end=end: wa.at[yy, :, core, pl.ds(16 + begin, end - begin)],
            lambda yy, begin=begin, end=end: theirs_a.at[yy, :, pl.ds(begin, end - begin)],
            far_a.at[:, :, pl.ds(begin // 2, (end - begin) // 2)], near_a.at[:, :, pl.ds(begin, end - begin)],
        )
        for begin, end in FIRST_PIECES
    ]
    sum8.relay_across()
    step_b(4)
    step_c(3)
    first_core.wait_recv()
    for piece in scatter_q:
        piece.step_a()
    sum8.relay_near()
    step_b(5)
    step_c(4)
    step_d(0)
    scatter_q[0].step_b()
    step_c(5)
    sum8.wait()
    given = sum8.total()
    grad, normed = norm_back(x_ref[...].astype(F32), given, gains[0:1])
    dtok_ref[...] = gmid_ref[...] + grad
    gain_sum = jnp.sum(given * normed, axis=0, keepdims=True)
    bias_sum = jnp.sum(given, axis=0, keepdims=True)
    bias_rows = jnp.concatenate([bias[:, i * 128 : (i + 1) * 128] for i in range(6)], axis=0)
    small_out[:, 4:10] = jnp.broadcast_to(bias_rows[None], (16, 6, 128))
    small_out[:, 10:16] = jnp.zeros((16, 6, 128), F32)
    for i in range(16):
        lanes = slice(i * 128, (i + 1) * 128)
        small_out[i, 0:1] = gain_sum[:, lanes]
        small_out[i, 1:2] = bias_sum[:, lanes]
        small_out[i, 2:4] = ln2_ref[0:2, lanes]
    copies = [
        net.send(small_out.at[place[0]], small_in.at[i], place) for i, place in enumerate(across_f)
    ]
    scatter_q[1].step_b()
    z_q = []
    for piece, (begin, end) in zip(scatter_q, FIRST_PIECES):
        piece.step_c()
        lines = pl.ds(begin, end - begin)
        z_q.append(net.send(wa.at[y, 1 - zh, core, pl.ds(16 + begin, end - begin)], by_z_a.at[lines], "zh"))
    step_d(1)
    step_d(2)
    total = small_out[f]
    for i, copy in enumerate(copies):
        copy.wait_recv()
        total = total + small_in[i]
    small_tp[...] = total
    copies = [net.send(small_tp.at[pl.ds(0, 8)], small_got.at[j], place) for j, place in enumerate(across_t)]
    for copy in z_q:
        copy.wait_recv()

    da_ref[...] = wa[y, zh, core, pl.ds(16, 1024)].astype(F32) + by_z_a[...].astype(F32)
    row_id = lax.broadcasted_iota(jnp.int32, (8, 128), 0)
    total = small_tp[0:8]
    for j, copy in enumerate(copies):
        copy.wait_recv()
        total = total + jnp.where(row_id < 4, small_got[j], 0.0)
    small_ref[0:8] = total
    small_ref[8:16] = small_tp[8:16]
    net.finish()


def k3(x, lens, wa, gmid, middle, down, ln2, grads, normed, q, k, v, att):
    shapes = [
        ((128, 2048), BF16, VM), ((128, 2048), F32, VM), ((3, ROWS_M, 128), F32, VM), ((1024, 128), F32, VM),
        ((16, 128), F32, VM), ((6, 4, 2, ROWS_M, 128), BF16, AN),
    ]
    scratch = [
        ((1024, 256), BF16), ((1024, 256), BF16), ((1024, 256), BF16), ((1024, 256), BF16),
        ((4, 2, 2, ROWS_A, 128), BF16), ((8, 128, 2048), BF16), ((8, 128, 2048), BF16), ((3, 128, 2048), BF16),
        ((8, 64, 2048), BF16), ((2, 128, 2048), BF16), ((2, 64, 2048), BF16),
        ((128, 2048), BF16), ((8, 2048), F32), ((1024, 256), BF16), ((1024, 256), F32), ((1024, 256), F32),
        ((1024, 768), BF16), ((768, 1024), BF16), ((1024, 128), jnp.int32), ((1024, 128), F32), ((1024, 128), F32),
        ((6, 4, 2, ROWS_M, 128), BF16), ((2, 4, 2, ROWS_M, 128), BF16), ((6, 2, 2, ROWS_M // 2, 128), BF16),
        ((6, 2, 2, ROWS_M, 128), BF16), ((3, 3, ROWS_M, 128), BF16), ((4, 2, 1024, 128), BF16),
        ((2, 2, 512, 128), BF16), ((2, 2, 1024, 128), BF16),
        ((1024, 128), BF16), ((16, 16, 128), F32), ((15, 16, 128), F32), ((16, 128), F32), ((7, 8, 128), F32),
    ]
    return pl.pallas_call(
        k3_kernel,
        out_shape=[jax.ShapeDtypeStruct(s, d) for s, d, _ in shapes],
        in_specs=[VM, SM, AN, VM, AN, AN, VM, AN, AN, AN, AN, AN, AN],
        out_specs=[m for _, _, m in shapes],
        scratch_shapes=[pltpu.VMEM(s, d) for s, d in scratch]
        + [pltpu.SemaphoreType.DMA((160,)), pltpu.SemaphoreType.DMA((160,)), pltpu.SemaphoreType.DMA((24,))],
        compiler_params=pltpu.CompilerParams(
            collective_id=3, has_side_effects=True, vmem_limit_bytes=63 * MIB
        ),
        name="attend_back_sum_gradients",
    )(
        x, lens, wa.reshape(4, 2, 2, ROWS_A, 128), gmid, middle, down, ln2,
        grads.reshape(3, 2, 4, 2, 2, ROWS_M, 128), normed, q, k, v, att,
    )


def finish_kernel(
    out_in, dtok_in, dm_in, da_in, small_in,
    out_ref, dtok_ref, gain1, bias1, dqkv, dout, gain2, bias2, dgate, dup, ddown,
):
    out_ref[...] = out_in[...]
    dtok_ref[...] = dtok_in[...]
    for i, ref in enumerate((gain1, bias1, gain2, bias2)):
        ref[...] = small_in[i : i + 1]
    for j in range(3):
        for part in range(2):
            lanes = slice(part * 128, (part + 1) * 128)
            dqkv[j, :, lanes] = da_in[j * 256 + part * 128 : j * 256 + (part + 1) * 128].T
    dout[...] = da_in[768:1024]
    dgate[...] = dm_in[0]
    dup[...] = dm_in[1]
    ddown[...] = dm_in[2]


def finish(out, d_tokens, dm, da, small):
    shapes = [
        ((128, 2048), BF16), ((128, 2048), F32), ((1, 128), F32), ((1, 128), F32), ((3, 128, 256), F32), ((256, 128), F32),
        ((1, 128), F32), ((1, 128), F32), ((ROWS_M, 128), F32), ((ROWS_M, 128), F32), ((ROWS_M, 128), F32),
    ]
    return pl.pallas_call(
        finish_kernel,
        out_shape=[jax.ShapeDtypeStruct(s, d) for s, d in shapes],
        in_specs=[VM] * 5,
        out_specs=[VM] * 11,
        compiler_params=pltpu.CompilerParams(vmem_limit_bytes=63 * MIB),
        name="lay_out_gradients",
    )(out, d_tokens, dm, da, small)


def local(
    tokens, seq_lens, ln1_gain, ln1_bias, w_qkv, b_qkv, w_out, ln2_gain, ln2_bias, w_gate, w_up, w_down, cotangent
):
    small = small_rows(ln1_gain, ln1_bias, b_qkv, ln2_gain, ln2_bias)
    normed, wa, wg, cotg, q, k, v, att = k1(
        tokens, seq_lens, small, jnp.transpose(w_qkv, (1, 0, 2)), w_out, w_gate.T, cotangent
    )
    middle, gmid, down, grads, ln2 = k2(tokens, att, wa, wg, w_up.T, w_down, cotangent, cotg)
    out, d_tokens, dm, da, small, _ = k3(
        tokens, seq_lens, wa, gmid, middle, down, ln2, grads, normed, q, k, v, att
    )
    d_bias = lax.dynamic_slice_in_dim(
        small[4:10].reshape(3, 4, HEAD_DIM), lax.axis_index("fsdp") * 4, 4, axis=2
    )
    out, d_tokens, gain1, bias1, dqkv, dout, gain2, bias2, dgate, dup, ddown = finish(out, d_tokens, dm, da, small)
    return (
        out, d_tokens, gain1[0], bias1[0], jnp.transpose(dqkv, (1, 0, 2)), d_bias, dout, gain2[0], bias2[0], dgate.T, dup.T, ddown,
    )


def solution(mesh):
    placed = (
        P(("fsdp", "tp"), None),
        P("fsdp", None),
        P("fsdp"),
        P("fsdp"),
        P("fsdp", None, "tp"),
        P(None, "tp", "fsdp"),
        P("tp", "fsdp"),
        P("fsdp"),
        P("fsdp"),
        P("fsdp", "tp"),
        P("fsdp", "tp"),
        P("tp", "fsdp"),
        P(("fsdp", "tp"), None),
    )
    return jax.shard_map(
        local,
        mesh=mesh,
        in_specs=placed,
        out_specs=(
            P(("fsdp", "tp"), None),
            P(("fsdp", "tp"), None),
            P("fsdp"),
            P("fsdp"),
            P("fsdp", None, "tp"),
            P(None, "tp", "fsdp"),
            P("tp", "fsdp"),
            P("fsdp"),
            P("fsdp"),
            P("fsdp", "tp"),
            P("fsdp", "tp"),
            P("tp", "fsdp"),
        ),
        check_vma=False,
    )
```

```python
import math

import jax
import jax.numpy as jnp
import numpy as np
from jax import lax
from jax.experimental import pallas as pl
from jax.experimental.pallas import tpu as pltpu
from jax.sharding import PartitionSpec as P

F32 = jnp.float32
BF16 = jnp.bfloat16
HEAD_DIM = 64
ROT = 16
EPS = 1e-05
ROPE_BASE = 10000.0
MASKED = -1e30
SCALE = HEAD_DIM**-0.5
ROWS_A = 1040
ROWS_Q = 784
ROWS_M = 704
MIB = 2**20


def nt(a, b):
    return lax.dot_general(a, b, (((1,), (1,)), ((), ())), preferred_element_type=F32)


def nn(a, b):
    return lax.dot_general(a, b, (((1,), (0,)), ((), ())), preferred_element_type=F32)


class Net:
    def __init__(self, send_sems, recv_sems, local_sems):
        f, t = lax.axis_index("fsdp"), lax.axis_index("tp")
        self.f, self.t = f, t
        self.x, self.zl = t // 2, lax.rem(t, 2)
        self.send_sems, self.recv_sems, self.local_sems = send_sems, recv_sems, local_sems
        self.started, self.pending, self.locals = 0, [], 0

    def tx(self, step, flip=0):
        zl = 1 - self.zl if flip else self.zl
        return lax.rem(self.x + step, 4) * 2 + zl

    def fy(self, f, step):
        return lax.rem(f + 4 * step, 16)

    def peer(self, name):
        if not isinstance(name, str):
            return name
        f, t = self.f, self.t
        core = f + 1 - 2 * lax.rem(f, 2)
        high = f + 2 - 4 * lax.rem(f // 2, 2)
        return {
            "xp": (f, self.tx(1)),
            "xm": (f, self.tx(3)),
            "zl": (f, self.tx(0, 1)),
            "zh": (high, t),
            "zo": (high, self.tx(0, 1)),
            "yp": (self.fy(f, 1), t),
            "ym": (self.fy(f, 3), t),
            "c": (core, t),
        }[name]

    def greet(self, names):
        barrier = pltpu.get_barrier_semaphore()
        for name in names:
            pl.semaphore_signal(
                barrier, inc=1, device_id=self.peer(name), device_id_type=pl.DeviceIdType.MESH
            )
        pl.semaphore_wait(barrier, len(names))

    def send(self, src, dst, name):
        k = self.started
        copy = pltpu.make_async_remote_copy(
            src_ref=src,
            dst_ref=dst,
            send_sem=self.send_sems.at[k],
            recv_sem=self.recv_sems.at[k],
            device_id=self.peer(name),
            device_id_type=pl.DeviceIdType.MESH,
        )
        copy.start()
        self.started += 1
        self.pending.append(copy)
        return copy

    def move(self, src, dst):
        copy = pltpu.make_async_copy(src, dst, self.local_sems.at[self.locals])
        copy.start()
        self.locals += 1
        return copy

    def settle(self, copies):
        for copy in copies:
            copy.wait_send()
        done = {id(copy) for copy in copies}
        self.pending = [copy for copy in self.pending if id(copy) not in done]

    def finish(self):
        for copy in self.pending:
            copy.wait_send()
        self.pending = []


class GatherTp:
    def __init__(self, net, src, buf):
        self.net, self.buf, self.src = net, buf, src
        half = src.shape[0] // 2
        self.lo, self.hi = pl.ds(0, half), pl.ds(half, half)

    def slot(self, step, flip=0):
        zl = 1 - self.net.zl if flip else self.net.zl
        return zl * 4 + lax.rem(self.net.x + step, 4)

    def pass_on(self, slot, rows, name):
        return self.net.send(self.buf.at[slot, rows], self.buf.at[slot, rows], name)

    def start(self):
        net, lo, hi = self.net, self.lo, self.hi
        own = self.slot(0)
        self.own = net.move(self.src, self.buf.at[own])
        self.xp_lo = net.send(self.src.at[lo], self.buf.at[own, lo], "xp")
        self.xm_hi = net.send(self.src.at[hi], self.buf.at[own, hi], "xm")
        self.xp_hi = net.send(self.src.at[hi], self.buf.at[own, hi], "xp")
        self.xm_lo = net.send(self.src.at[lo], self.buf.at[own, lo], "xm")

    def start_z(self):
        self.z = self.net.send(self.src, self.buf.at[self.slot(0)], "zl")

    def relay(self):
        lo, hi = self.lo, self.hi
        left, right = self.slot(3), self.slot(1)
        self.xp_lo.wait_recv()
        self.fwd_p = self.pass_on(left, lo, "xp")
        self.xm_hi.wait_recv()
        self.fwd_m = self.pass_on(right, hi, "xm")
        self.xp_hi.wait_recv()
        self.za_p = self.pass_on(left, hi, "zl")
        self.xm_lo.wait_recv()
        self.za_m = self.pass_on(right, lo, "zl")

    def relay_z(self):
        across = self.slot(0, 1)
        self.z.wait_recv()
        self.zb_p = self.pass_on(across, self.lo, "xp")
        self.zb_m = self.pass_on(across, self.hi, "xm")

    def relay_far(self):
        self.zb_p.wait_recv()
        self.fz_p = self.pass_on(self.slot(3, 1), self.lo, "xp")
        self.zb_m.wait_recv()
        self.fz_m = self.pass_on(self.slot(1, 1), self.hi, "xm")

    def plane(self):
        self.fwd_p.wait_recv()
        self.fwd_m.wait_recv()
        self.own.wait()

    def rest(self):
        for copy in (self.za_p, self.za_m, self.fz_p, self.fz_m):
            copy.wait_recv()


class GatherX:
    def __init__(self, net, src, buf):
        self.net, self.buf, self.src = net, buf, src
        self.half = src.shape[0] // 2

    def slot(self, step):
        return lax.rem(self.net.x + step, 4)

    def start(self):
        net, h = self.net, self.half
        lo, hi = pl.ds(0, h), pl.ds(h, h)
        own = self.slot(0)
        self.own = net.move(self.src, self.buf.at[own])
        self.xp_lo = net.send(self.src.at[lo], self.buf.at[own, lo], "xp")
        self.xm_hi = net.send(self.src.at[hi], self.buf.at[own, hi], "xm")
        self.xp_hi = net.send(self.src.at[hi], self.buf.at[own, hi], "xp")
        self.xm_lo = net.send(self.src.at[lo], self.buf.at[own, lo], "xm")

    def relay(self):
        net, h = self.net, self.half
        lo, hi = pl.ds(0, h), pl.ds(h, h)
        left, right = self.slot(3), self.slot(1)
        self.xp_lo.wait_recv()
        self.fwd_p = net.send(self.buf.at[left, lo], self.buf.at[left, lo], "xp")
        self.xm_hi.wait_recv()
        self.fwd_m = net.send(self.buf.at[right, hi], self.buf.at[right, hi], "xm")

    def near(self):
        self.xp_hi.wait_recv()
        self.xm_lo.wait_recv()

    def far(self):
        self.fwd_p.wait_recv()
        self.fwd_m.wait_recv()


class GatherW:
    def __init__(self, net, src, buf, wide, offset=0):
        self.net, self.src, self.buf, self.wide, self.offset = net, src, buf, wide, offset
        self.half = src.shape[0] // 32 * 16
        f = net.f
        high = f + 2 - 4 * lax.rem(f // 2, 2)
        self.sources = [((0, f), None), ((0, high), "zh")]
        if wide:
            self.sources += [((1, f), "zl"), ((1, high), "zo")]

    def at(self, key, step, rows=None):
        flip, f = key
        f = self.net.fy(f, step)
        start, size = (0, self.src.shape[0]) if rows is None else rows
        rows = pl.ds(self.offset + start, size)
        if self.wide:
            side = 1 - self.net.zl if flip else self.net.zl
            place = (f,) if len(self.buf.shape) == 4 else (f // 4, lax.rem(f // 2, 2), lax.rem(f, 2))
            return self.buf.at[(side, *place, rows)]
        return self.buf.at[f, rows]

    def pass_on(self, key, step, name, rows=None, src=None):
        here = self.at(key, step, rows)
        return self.net.send(here if src is None else src, here, name)

    def start(self):
        net, src = self.net, self.src
        own = (0, net.f)
        self.own = net.move(src, self.at(own, 0))
        self.by_z = [
            self.pass_on(own, 0, name, src=src) for _, name in self.sources if name is not None
        ]
        self.by_y = [(self.pass_on(own, 0, "yp", src=src), self.pass_on(own, 0, "ym", src=src))]
        self.by_c = [self.pass_on(own, 0, "c", src=src)]
        self.by_y2 = []

    def relay_z(self):
        for copy, (key, _) in zip(self.by_z, self.sources[1:]):
            copy.wait_recv()
            self.by_y.append((self.pass_on(key, 0, "yp"), self.pass_on(key, 0, "ym")))
            self.by_c.append(self.pass_on(key, 0, "c"))

    def relay_y(self, i):
        key, h = self.sources[i][0], self.half
        up, down = self.by_y[i]
        rows = self.src.shape[0]
        up.wait_recv()
        fwd_up = self.pass_on(key, 3, "yp", (0, h))
        down.wait_recv()
        fwd_down = self.pass_on(key, 1, "ym", (h, rows - h))
        self.by_c.append(self.pass_on(key, 3, "c"))
        self.by_c.append(self.pass_on(key, 1, "c"))
        self.by_y2.append((fwd_up, fwd_down))

    def relay_far(self, i):
        for copy in self.by_y2[i]:
            copy.wait_recv()
        self.by_c.append(self.pass_on(self.sources[i][0], 2, "c"))

    def finish(self):
        self.own.wait()
        for copy in self.by_c:
            copy.wait_recv()


def norm_rows(x, gain, bias):
    center = x - jnp.mean(x, axis=-1, keepdims=True)
    spread = jnp.mean(center * center, axis=-1, keepdims=True)
    return center * lax.rsqrt(spread + EPS) * gain + bias


def position_tables(lens_ref, begin_ref, cos_ref, sin_ref):
    rows = begin_ref.shape[0]
    slot = lax.broadcasted_iota(jnp.int32, (rows, 128), 0)
    begin = jnp.zeros((rows, 128), jnp.int32)
    end = jnp.int32(0)
    for i in range(lens_ref.shape[1]):
        length = lens_ref[0, i]
        end = end + length
        begin = begin + jnp.where(slot >= end, length, 0)
    begin_ref[...] = begin
    lane = lax.rem(lax.broadcasted_iota(jnp.int32, (1, 128), 1), HEAD_DIM)
    which = lax.rem(lane, ROT // 2)
    frequency = jnp.zeros((1, 128), F32)
    for j in range(ROT // 2):
        value = float(np.exp(np.float32(j) * np.float32(-2.0 * math.log(ROPE_BASE) / ROT)))
        frequency = jnp.where(which == j, value, frequency)
    angle = (slot - begin).astype(F32) * frequency
    turns = jnp.floor(angle * (2.0 / math.pi) + 0.5)
    r = angle - turns * 1.5703125 - turns * 4.837512969970703125e-4 - turns * 7.54978995489188216e-8
    z = r * r
    sine = ((-1.9515295891e-4 * z + 8.3321608736e-3) * z - 1.6666654611e-1) * z * r + r
    cosine = (
        ((2.443315711809948e-5 * z - 1.388731625493765e-3) * z + 4.166664568298827e-2) * z * z
        - 0.5 * z
        + 1.0
    )
    quadrant = turns - 4.0 * jnp.floor(turns * 0.25)
    odd = (quadrant == 1.0) | (quadrant == 3.0)
    cos_all = jnp.where(odd, sine, cosine)
    cos_all = jnp.where((quadrant == 1.0) | (quadrant == 2.0), -cos_all, cos_all)
    sin_all = jnp.where(odd, cosine, sine)
    sin_all = jnp.where(quadrant >= 2.0, -sin_all, sin_all)
    cos_ref[...] = jnp.where(lane < ROT, cos_all, 1.0)
    sin_ref[...] = jnp.where(lane < ROT, sin_all, 0.0)


def turn(values, cos, sin, direction):
    lane = lax.rem(lax.broadcasted_iota(jnp.int32, (1, 256), 1), HEAD_DIM)
    cos = jnp.concatenate([cos, cos], axis=1)
    sin = jnp.concatenate([sin, sin], axis=1) * direction
    after = pltpu.roll(values, 256 - ROT // 2, 1)
    before = pltpu.roll(values, ROT // 2, 1)
    other = jnp.where(lane < ROT // 2, -after, before)
    return values * cos + other * sin


def head_mask(h):
    return lax.broadcasted_iota(jnp.int32, (1, 256), 1) // HEAD_DIM == h


def scores_of(q_block, keys, begin, first, h):
    rows, stop = q_block.shape[0], keys.shape[0]
    q_head = jnp.where(head_mask(h), q_block, jnp.zeros_like(q_block))
    scores = nt(q_head, keys)
    key_slot = lax.broadcasted_iota(jnp.int32, (rows, stop), 1)
    query_slot = lax.broadcasted_iota(jnp.int32, (rows, stop), 0) + first
    return jnp.where((key_slot >= begin) & (key_slot <= query_slot), scores, MASKED)


def flip_into(ref, first, source):
    columns = source.shape[1]
    for begin in range(0, columns, 128):
        end = min(begin + 128, columns)
        ref[first + begin : first + end] = source[:, begin:end].T


def k1_kernel(
    x_ref, lens_ref, small_ref, w_qkv, w_out, pack_g, cot_ref,
    normed_hbm, wa_hbm, wg_hbm, cotg_hbm, q_hbm, k_hbm, v_hbm, att_hbm,
    normed_ref, wa_ref, wg_ref, cotg_ref, q_ref, k_ref, v_ref, att_ref,
    pack_a, raw, gains, biases, begin_ref, cos_ref, sin_ref, send_sems, recv_sems, local_sems,
):
    net = Net(send_sems, recv_sems, local_sems)
    pack_a[0:16] = small_ref[...]
    for j in range(3):
        flip_into(pack_a, 16 + 256 * j, w_qkv.at[j])
    net.greet(["xp", "xm", "zl", "zh", "zo", "yp", "ym", "c"])
    tokens = GatherTp(net, x_ref, raw)
    wa = GatherW(net, pack_a, wa_ref, False)
    wo = GatherW(net, w_out, wa_ref, False, ROWS_Q)
    wg = GatherW(net, pack_g, wg_ref, True)
    cot = GatherX(net, cot_ref, cotg_ref)
    wa.start()
    tokens.start()
    position_tables(lens_ref, begin_ref, cos_ref, sin_ref)
    wa.relay_z()
    tokens.start_z()
    wg.start()
    wa.relay_y(0)
    tokens.relay()
    wa.relay_far(0)
    wa.relay_y(1)
    wa.relay_far(1)
    tokens.relay_z()
    wa.finish()
    stores = []
    for f in range(16):
        small = wa_ref[f, 0:16].astype(F32)
        gains[0:2, f * 128 : (f + 1) * 128] = small[0:2]
        biases[0:16, :] = small if f == 0 else biases[0:16, :] + small

    def project(side):
        def norm_some(i, carry):
            values = raw[side * 4 + i].astype(F32)
            normed_ref[i * 2 + side] = norm_rows(values, gains[0:1, :], gains[1:2, :]).astype(BF16)
            return carry

        lax.fori_loop(0, 4, norm_some, 0)

        def some_rows(i, carry):
            chunks = [2 * (2 * i + n) + side for n in range(2)]
            given = jnp.concatenate([normed_ref[chunk] for chunk in chunks], axis=0)
            rows = [pl.ds(pl.multiple_of(chunk * 128, 128), 128) for chunk in chunks]
            cos = jnp.concatenate([cos_ref[r] for r in rows], axis=0)
            sin = jnp.concatenate([sin_ref[r] for r in rows], axis=0)
            for j, out in enumerate((q_ref, k_ref, v_ref)):
                lines = slice(16 + 256 * j, 16 + 256 * (j + 1))
                total = nt(given, jnp.concatenate([wa_ref[f, lines] for f in range(16)], axis=1))
                total = total + jnp.concatenate([biases[4 + 2 * j : 5 + 2 * j], biases[5 + 2 * j : 6 + 2 * j]], axis=1)
                if j < 2:
                    total = turn(total, cos, sin, 1.0)
                for n in range(2):
                    out[rows[n]] = total[n * 128 : (n + 1) * 128].astype(BF16)
            return carry

        lax.fori_loop(0, 2, some_rows, 0)

    tokens.plane()
    wg.relay_y(0)
    project(net.zl)
    tokens.relay_far()
    wo.start()
    wg.relay_z()
    cot.start()
    wg.relay_far(0)
    tokens.rest()
    project(1 - net.zl)
    stores += [net.move(normed_ref, normed_hbm), net.move(q_ref, q_hbm)]
    stores += [net.move(k_ref, k_hbm), net.move(v_ref, v_hbm)]
    wg.relay_y(1)
    for block in range(4):
        first, stop = block * 256, (block + 1) * 256
        q_block = q_ref[first:stop] * jnp.asarray(SCALE, BF16)
        begin = begin_ref[first:stop, 0:1]
        mixed = jnp.zeros((256, 256), F32)
        for h in range(4):
            scores = scores_of(q_block, k_ref[0:stop], begin, first, h)
            weights = jnp.exp(scores - jnp.max(scores, axis=-1, keepdims=True))
            probs = (weights * (1.0 / jnp.sum(weights, axis=-1, keepdims=True))).astype(BF16)
            mixed = jnp.where(head_mask(h), nn(probs, v_ref[0:stop]), mixed)
        att_ref[first:stop] = mixed.astype(BF16)
        if block == 1:
            wg.relay_y(2)
            wo.relay_z()
        if block == 2:
            wg.relay_y(3)
            wg.relay_far(1)
            wo.relay_y(0)
    stores.append(net.move(att_ref, att_hbm))
    cot.relay()
    wo.relay_y(1)
    wg.relay_far(2)
    wg.relay_far(3)
    wo.relay_far(0)
    wo.relay_far(1)
    wg.finish()
    stores.append(net.move(wg_ref, wg_hbm))
    wo.finish()
    stores.append(net.move(wa_ref, wa_hbm))
    cot.own.wait()
    cot.near()
    cot.far()
    stores.append(net.move(cotg_ref, cotg_hbm))
    for copy in stores:
        copy.wait()
    net.finish()


def hbm(shape, dtype=BF16):
    return jax.ShapeDtypeStruct(shape, dtype)


VM = pl.BlockSpec(memory_space=pltpu.VMEM)
SM = pl.BlockSpec(memory_space=pltpu.SMEM)
AN = pl.BlockSpec(memory_space=pl.ANY)


def k1(x, lens, small, w_qkv, w_out, pack_g, cot):
    shapes = [
        (8, 128, 2048), (16, ROWS_A, 128), (2, 16, ROWS_M, 128), (4, 128, 2048),
        (1024, 256), (1024, 256), (1024, 256), (1024, 256),
    ]
    return pl.pallas_call(
        k1_kernel,
        out_shape=[hbm(s) for s in shapes],
        in_specs=[VM, SM, VM, VM, VM, VM, VM],
        out_specs=[AN] * 8,
        scratch_shapes=[pltpu.VMEM(s, BF16) for s in shapes + [(ROWS_Q, 128)]]
        + [
            pltpu.VMEM((8, 128, 2048), BF16),
            pltpu.VMEM((8, 2048), F32),
            pltpu.VMEM((16, 128), F32),
            pltpu.VMEM((1024, 128), jnp.int32),
            pltpu.VMEM((1024, 128), F32),
            pltpu.VMEM((1024, 128), F32),
            pltpu.SemaphoreType.DMA((160,)),
            pltpu.SemaphoreType.DMA((160,)),
            pltpu.SemaphoreType.DMA((16,)),
        ],
        compiler_params=pltpu.CompilerParams(
            collective_id=1, has_side_effects=True, vmem_limit_bytes=56 * MIB
        ),
        name="gather_project_attend",
    )(x, lens, small, w_qkv, w_out, pack_g, cot)


def small_rows(ln1_gain, ln1_bias, b_qkv, ln2_gain, ln2_bias):
    spread = jnp.zeros((3, 4, 16, 4), BF16)
    spread = lax.dynamic_update_slice(
        spread, b_qkv.reshape(3, 4, 1, 4), (0, 0, lax.axis_index("fsdp"), 0)
    ).reshape(6, 128)
    rows = lax.broadcasted_iota(jnp.int32, (16, 128), 0)
    small = jnp.pad(spread, ((4, 6), (0, 0)))
    for i, row in enumerate((ln1_gain, ln1_bias, ln2_gain, ln2_bias)):
        small = jnp.where(rows == i, row[None, :], small)
    return small


class ScatterTp:
    def __init__(self, net, parts, got, got_half):
        self.net, self.parts, self.got, self.got_half = net, parts, got, got_half
        half = parts.shape[1] // 2
        self.lo, self.hi = pl.ds(0, half), pl.ds(half, half)

    slot = GatherTp.slot

    def half_to(self, slot, rows, name, place):
        return self.net.send(self.parts.at[slot, rows], self.got_half.at[place], name)

    def add(self, slot, rows, *places):
        total = self.parts[slot, rows].astype(F32)
        for place in places:
            total = total + self.got_half[place].astype(F32)
        self.parts[slot, rows] = total.astype(BF16)

    def start_side(self):
        lo, hi = self.lo, self.hi
        self.zx2 = [self.half_to(self.slot(2, 1), lo, "xm", 0), self.half_to(self.slot(2, 1), hi, "xp", 1)]
        self.by_z = [self.half_to(self.slot(3, 1), hi, "zl", 2), self.half_to(self.slot(1, 1), lo, "zl", 4)]

    def start_plane(self):
        net, parts, lo, hi = self.net, self.parts, self.lo, self.hi
        far, left, right = self.slot(2), self.slot(3), self.slot(1)
        self.x2 = [self.half_to(far, hi, "xm", 6), self.half_to(far, lo, "xp", 7)]
        self.near_m = [net.send(parts.at[left, lo], self.got.at[1, lo], "xm")]
        self.near_p = [net.send(parts.at[right, hi], self.got.at[2, hi], "xp")]

    def relay_side(self):
        lo, hi = self.lo, self.hi
        self.zx2[0].wait_recv()
        self.add(self.slot(3, 1), lo, 0)
        self.across = [self.half_to(self.slot(3, 1), lo, "xm", 3)]
        self.zx2[1].wait_recv()
        self.add(self.slot(1, 1), hi, 1)
        self.across.append(self.half_to(self.slot(1, 1), hi, "xp", 5))

    def relay_across(self):
        across = self.slot(0, 1)
        self.across[0].wait_recv()
        self.add(across, self.lo, 3)
        self.across[1].wait_recv()
        self.add(across, self.hi, 5)
        self.z_own = self.net.send(self.parts.at[across], self.got.at[0], "zl")

    def relay_near(self):
        net, parts, lo, hi = self.net, self.parts, self.lo, self.hi
        left, right = self.slot(3), self.slot(1)
        self.by_z[0].wait_recv()
        self.x2[0].wait_recv()
        self.add(left, hi, 2, 6)
        self.near_m.append(net.send(parts.at[left, hi], self.got.at[1, hi], "xm"))
        self.by_z[1].wait_recv()
        self.x2[1].wait_recv()
        self.add(right, lo, 4, 7)
        self.near_p.append(net.send(parts.at[right, lo], self.got.at[2, lo], "xp"))

    def wait(self):
        self.z_own.wait_recv()
        for copy in self.near_p + self.near_m:
            copy.wait_recv()

    def total(self):
        total = self.parts[self.slot(0)].astype(F32)
        for i in range(3):
            total = total + self.got[i].astype(F32)
        return total


class ScatterX:
    def __init__(self, net, parts, got, got_half):
        self.net, self.parts, self.got, self.got_half = net, parts, got, got_half
        self.half = parts.shape[1] // 2

    slot = GatherX.slot

    def add(self, slot, rows, arrived):
        total = self.parts[slot, rows].astype(F32) + arrived[...].astype(F32)
        self.parts[slot, rows] = total.astype(BF16)

    def start_far(self):
        net, h, parts = self.net, self.half, self.parts
        far = self.slot(2)
        self.half_p = net.send(parts.at[far, pl.ds(0, h)], self.got_half.at[0], "xp")
        self.half_m = net.send(parts.at[far, pl.ds(h, h)], self.got_half.at[1], "xm")

    def start_near(self):
        net, h, parts = self.net, self.half, self.parts
        right, left = self.slot(1), self.slot(3)
        self.near_p = [net.send(parts.at[right, pl.ds(h, h)], self.got.at[0, pl.ds(h, h)], "xp")]
        self.near_m = [net.send(parts.at[left, pl.ds(0, h)], self.got.at[1, pl.ds(0, h)], "xm")]

    def relay_near(self):
        net, h, parts = self.net, self.half, self.parts
        right, left = self.slot(1), self.slot(3)
        self.half_p.wait_recv()
        self.add(right, pl.ds(0, h), self.got_half.at[0])
        self.near_p.append(net.send(parts.at[right, pl.ds(0, h)], self.got.at[0, pl.ds(0, h)], "xp"))
        self.half_m.wait_recv()
        self.add(left, pl.ds(h, h), self.got_half.at[1])
        self.near_m.append(net.send(parts.at[left, pl.ds(h, h)], self.got.at[1, pl.ds(h, h)], "xm"))

    def wait(self):
        for copy in self.near_p + self.near_m:
            copy.wait_recv()

    def total(self):
        total = self.parts[self.slot(0)].astype(F32)
        return total + self.got[0].astype(F32) + self.got[1].astype(F32)


def side_by_side(ref, lead, lines, slabs):
    return jnp.concatenate([ref[(*lead, f, lines)] for f in slabs], axis=1)


TILES = ((0, 256), (256, 512), (512, 704))


def k2_kernel(
    x_ref, att_ref, wa_hbm, wg_hbm, pack_u, pack_d, cot_ref, cotg_hbm,
    middle_hbm, gmid_ref, down_hbm, grads_hbm, ln2_ref,
    wo, small_ref, middle_ref, down_ref, parts, got8, got8_half, gains, n2_own, n2, wg, wu, wd, cotg, gate, up, ghid, hid, gg, gu, got4, got4_half, flipped,
    send_sems, recv_sems, local_sems,
):
    net = Net(send_sems, recv_sems, local_sems)
    net.greet(["xp", "xm", "zl", "zh", "zo", "yp", "ym", "c"])
    wug = GatherW(net, pack_u, wu, True)
    wdg = GatherW(net, pack_d, wd, True)
    wdg.start()
    first = [net.move(wa_hbm.at[:, pl.ds(784, 256)], wo), net.move(wa_hbm.at[:, pl.ds(0, 16)], small_ref)]
    moves = [net.move(wg_hbm, wg), net.move(cotg_hbm, cotg)]
    for copy in first:
        copy.wait()
    sum8 = ScatterTp(net, parts, got8, got8_half)

    def attention_out(side):
        rows = [att_ref[pl.ds(pl.multiple_of((2 * i + side) * 128, 128), 128)] for i in range(4)]
        rows = jnp.concatenate(rows, axis=0)
        for pair in range(8):
            weight = side_by_side(wo, (), slice(0, 256), (2 * pair, 2 * pair + 1))
            part = nn(rows, weight).astype(BF16).reshape(4, 128, 256)
            parts[pl.ds(side * 4, 4), :, pair * 256 : (pair + 1) * 256] = part

    attention_out(1 - net.zl)
    sum8.start_side()
    attention_out(net.zl)
    for f in range(16):
        small = small_ref[f].astype(F32)
        gains[0:2, f * 128 : (f + 1) * 128] = small[2:4]
    sum8.start_plane()
    sum8.relay_side()
    wdg.relay_z()
    wug.start()
    wdg.relay_y(0)
    sum8.relay_across()
    for i in range(1, 4):
        wdg.relay_y(i)
    wug.relay_z()
    sum8.relay_near()
    for i in range(4):
        wdg.relay_far(i)
    wug.relay_y(0)
    sum8.wait()
    middle = x_ref[...].astype(F32) + sum8.total()
    middle_ref[...] = middle
    n2_own[...] = norm_rows(middle, gains[0:1], gains[1:2]).astype(BF16)
    gather = GatherX(net, n2_own, n2)
    gather.start()
    stores = [net.move(middle_ref, middle_hbm)]
    for copy in moves:
        copy.wait()
    for i in range(1, 4):
        wug.relay_y(i)
    wdg.finish()

    def rows_of(slot):
        return pl.ds(slot * 128 if isinstance(slot, int) else pl.multiple_of(slot * 128, 128), 128)

    def grad_hidden(slots):
        given = jnp.concatenate([cotg[slot] for slot in slots], axis=0)
        for side in range(2):
            for a, b in TILES:
                value = nt(given, side_by_side(wd, (side,), slice(a, b), range(16))).astype(BF16)
                for i, slot in enumerate(slots):
                    ghid[side, rows_of(slot), a:b] = value[i * 128 : (i + 1) * 128]

    def project(slots, weight, out):
        given = jnp.concatenate([n2[slot] for slot in slots], axis=0)
        for side in range(2):
            for a, b in TILES:
                value = nt(given, side_by_side(weight, (side,), slice(a, b), range(16)))
                for i, slot in enumerate(slots):
                    out[side, rows_of(slot), a:b] = value[i * 128 : (i + 1) * 128]

    def units(slots):
        for slot in slots:
            rows = rows_of(slot)
            for side in range(2):
                g, u = gate[side, rows], up[side, rows]
                gh = ghid[side, rows].astype(F32)
                sig = 1.0 / (1.0 + jnp.exp(-g))
                act = g * sig
                hid[side, rows] = (act * u).astype(BF16)
                gu[side, rows] = (gh * act).astype(BF16)
                gg[side, rows] = (gh * u * (sig + act * (1.0 - sig))).astype(BF16)

    grad_parts = parts.at[pl.ds(0, 4)]

    def back(slots):
        rows = [rows_of(slot) for slot in slots]
        given = [
            (jnp.concatenate([ref[side, r] for r in rows], axis=0), weight, side)
            for ref, weight in ((gg, wg), (gu, wu))
            for side in range(2)
        ]
        for pair in range(8):
            total = None
            for value, weight, side in given:
                term = nn(value, side_by_side(weight, (side,), slice(0, 704), (2 * pair, 2 * pair + 1)))
                total = term if total is None else total + term
            for i, slot in enumerate(slots):
                grad_parts[slot, :, pair * 256 : (pair + 1) * 256] = total[i * 128 : (i + 1) * 128].astype(BF16)

    own, right, far, left = (gather.slot(i) for i in range(4))
    grad_hidden([0, 1, 2, 3])
    gather.relay()
    gather.own.wait()
    project([own], wg, gate)
    for i in range(4):
        wug.relay_far(i)
    gather.near()
    project([right, left], wg, gate)
    gather.far()
    project([far], wg, gate)
    wug.finish()
    project([0, 1, 2, 3], wu, up)
    sum4 = ScatterX(net, grad_parts, got4, got4_half)
    net.finish()
    units([far])
    back([far])
    sum4.start_far()
    units([right, left])
    back([right, left])
    sum4.start_near()
    units([own])
    back([own])
    sum4.relay_near()

    def down(m, carry):
        rows = pl.ds(pl.multiple_of(m * 256, 256), 256)
        for pair in range(8):
            total = None
            for side in range(2):
                term = nn(hid[side, rows], side_by_side(wd, (side,), slice(0, 704), (2 * pair, 2 * pair + 1)))
                total = term if total is None else total + term
            down_ref[pl.ds(2 * m, 2), :, pair * 256 : (pair + 1) * 256] = total.astype(BF16).reshape(2, 128, 256)
        return carry

    lax.fori_loop(0, 2, down, 0)
    stores.append(net.move(down_ref, down_hbm))
    for k, (ref, given, weight) in enumerate(((gg, n2, wg), (gu, n2, wu), (hid, cotg, wd))):
        for side in range(2):
            flipped[...] = ref[side].T
            for pair in range(8):
                some = given[:, :, pair * 256 : (pair + 1) * 256].reshape(512, 256)
                product = nn(flipped[...], some).astype(BF16)
                weight[side, 2 * pair] = product[:, 0:128]
                weight[side, 2 * pair + 1] = product[:, 128:256]
            stores.append(net.move(weight.at[side], grads_hbm.at[k, side]))
    sum4.wait()

    given = sum4.total()
    grad, normed = norm_back(middle_ref[...], given, gains[0:1])
    gmid_ref[...] = cot_ref[...].astype(F32) + grad
    ln2_ref[0:1] = jnp.sum(given * normed, axis=0, keepdims=True)
    ln2_ref[1:2] = jnp.sum(given, axis=0, keepdims=True)
    ln2_ref[2:8] = jnp.zeros((6, 2048), F32)
    for copy in stores:
        copy.wait()
    net.finish()


def norm_back(x, given, gain):
    center = x - jnp.mean(x, axis=-1, keepdims=True)
    scale = lax.rsqrt(jnp.mean(center * center, axis=-1, keepdims=True) + EPS)
    normed = center * scale
    q = given * gain
    grad = scale * (
        q - jnp.mean(q, axis=-1, keepdims=True) - normed * jnp.mean(q * normed, axis=-1, keepdims=True)
    )
    return grad, normed


def k2(x, att, wa, wg, pack_u, pack_d, cot, cotg):
    shapes = [
        ((128, 2048), F32, AN), ((128, 2048), F32, VM), ((4, 128, 2048), BF16, AN),
        ((3, 2, 16, ROWS_M, 128), BF16, AN), ((8, 2048), F32, VM),
    ]
    wide, tall = (2, 16, ROWS_M, 128), (2, 512, ROWS_M)
    return pl.pallas_call(
        k2_kernel,
        out_shape=[jax.ShapeDtypeStruct(s, d) for s, d, _ in shapes],
        in_specs=[VM, VM, AN, AN, VM, VM, VM, AN],
        out_specs=[m for _, _, m in shapes],
        scratch_shapes=[
            pltpu.VMEM((16, 256, 128), BF16),
            pltpu.VMEM((16, 16, 128), BF16),
            pltpu.VMEM((128, 2048), F32),
            pltpu.VMEM((4, 128, 2048), BF16),
            pltpu.VMEM((8, 128, 2048), BF16),
            pltpu.VMEM((3, 128, 2048), BF16),
            pltpu.VMEM((8, 64, 2048), BF16),
            pltpu.VMEM((8, 2048), F32),
            pltpu.VMEM((128, 2048), BF16),
            pltpu.VMEM((4, 128, 2048), BF16),
            pltpu.VMEM(wide, BF16),
            pltpu.VMEM(wide, BF16),
            pltpu.VMEM(wide, BF16),
            pltpu.VMEM((4, 128, 2048), BF16),
            pltpu.VMEM(tall, F32),
            pltpu.VMEM(tall, F32),
            pltpu.VMEM(tall, BF16),
            pltpu.VMEM(tall, BF16),
            pltpu.VMEM(tall, BF16),
            pltpu.VMEM(tall, BF16),
            pltpu.VMEM((2, 128, 2048), BF16),
            pltpu.VMEM((2, 64, 2048), BF16),
            pltpu.VMEM((ROWS_M, 512), BF16),
            pltpu.SemaphoreType.DMA((160,)),
            pltpu.SemaphoreType.DMA((160,)),
            pltpu.SemaphoreType.DMA((16,)),
        ],
        compiler_params=pltpu.CompilerParams(
            collective_id=2, has_side_effects=True, vmem_limit_bytes=63 * MIB
        ),
        name="project_norm_feed_forward",
    )(x, att, wa, wg, pack_u, pack_d, cot, cotg)


def tn(a, b):
    return lax.dot_general(a, b, (((0,), (0,)), ((), ())), preferred_element_type=F32)


class ScatterW:
    def __init__(self, net, rows, own, theirs, far, near):
        self.net, self.rows, self.half = net, rows, rows // 2
        self.own, self.theirs, self.far, self.near = own, theirs, far, near
        self.y = net.f // 4

    def at(self, step):
        return lax.rem(self.y + step, 4)

    def add(self, target, rows, *arrived):
        if len(arrived) == 1:
            target[:, rows] = target[:, rows] + arrived[0]
            return
        total = target[:, rows].astype(F32)
        for value in arrived:
            total = total + value.astype(F32)
        target[:, rows] = total.astype(BF16)

    def step_a(self):
        net, h, rows = self.net, self.half, self.rows
        lo, hi = pl.ds(0, h), pl.ds(h, rows - h)
        own, y = self.own, self.at

        def add(step):
            ref = self.theirs(y(step))
            self.add(own(y(step)), pl.ds(0, rows), ref[...])

        add(2)
        self.far_p = net.send(own(y(2)).at[:, lo], self.far.at[0], "yp")
        self.far_m = net.send(own(y(2)).at[:, hi], self.far.at[1], "ym")
        add(1)
        self.near_p = [net.send(own(y(1)).at[:, hi], self.near.at[0, :, hi], "yp")]
        add(3)
        self.near_m = [net.send(own(y(3)).at[:, lo], self.near.at[1, :, lo], "ym")]
        add(0)

    def step_b(self):
        net, h, rows = self.net, self.half, self.rows
        lo, hi = pl.ds(0, h), pl.ds(h, rows - h)
        own, y, far = self.own, self.at, self.far
        self.far_p.wait_recv()
        self.add(own(y(1)), lo, far[0])
        self.near_p.append(net.send(own(y(1)).at[:, lo], self.near.at[0, :, lo], "yp"))
        self.far_m.wait_recv()
        self.add(own(y(3)), hi, far[1])
        self.near_m.append(net.send(own(y(3)).at[:, hi], self.near.at[1, :, hi], "ym"))

    def step_c(self):
        for copy in self.near_p + self.near_m:
            copy.wait_recv()
        near = self.near
        self.add(self.own(self.y), pl.ds(0, self.rows), near[0], near[1])


FIRST_PIECES = ((384, 1024), (0, 384))


def k3_kernel(
    x_ref, lens_ref, wa_hbm, gmid_ref, middle_hbm, down_hbm, ln2_ref, grads_hbm, normed_hbm, q_hbm, k_hbm, v_hbm, att_hbm,
    out_ref, dtok_ref, dm_ref, da_ref, small_ref, theirs_hbm,
    q_ref, k_ref, v_ref, att_ref, wa, gb, parts, got8, got8_half, got4, got4_half, g_own, gains, ga, dk, dv, gproj, flipped, begin_ref, cos_ref, sin_ref,
    sums, stage, far_m, near_m, by_z, theirs_a, far_a, near_a, by_z_a, small_out, small_in, small_tp, small_got,
    send_sems, recv_sems, local_sems,
):
    net = Net(send_sems, recv_sems, local_sems)
    f, t = net.f, net.t
    core, zh, y = lax.rem(f, 2), lax.rem(f // 2, 2), f // 4
    across_f = [(lax.rem(f + i, 16), t) for i in range(1, 16)]
    across_t = [(f, lax.rem(t + j, 8)) for j in range(1, 8)]
    net.greet(across_f + across_t + ["zo"])
    load_wa = net.move(wa_hbm, wa)
    units = [(k, flip) for k in range(3) for flip in (1, 0)]
    sides = (net.zl, 1 - net.zl)
    to_core, load_sums = [], []
    for u, (k, flip) in enumerate(units):
        there = stage.at[u] if u < 2 else theirs_hbm.at[u]
        to_core.append(net.send(grads_hbm.at[k, sides[flip], :, :, 1 - core], there, "c"))
        load_sums.append(net.move(grads_hbm.at[k, sides[flip], :, :, core], sums.at[u]))
    down = parts.at[pl.ds(net.zl * 4, 4)]
    load_down = net.move(down_hbm, down)
    load_rest = [net.move(q_hbm, q_ref), net.move(k_hbm, k_ref), net.move(v_hbm, v_ref), net.move(att_hbm, att_ref)]
    load_middle = net.move(middle_hbm, dtok_ref)

    def cast(i, carry):
        rows = pl.ds(pl.multiple_of(i * 32, 32), 32)
        g_own[rows] = gmid_ref[rows].astype(BF16)
        return carry

    lax.fori_loop(0, 4, cast, 0)
    gather = GatherTp(net, g_own, gb)
    gather.start()
    gather.start_z()
    position_tables(lens_ref, begin_ref, cos_ref, sin_ref)
    load_wa.wait()
    for i in range(16):
        small = wa[i // 4, i // 2 % 2, i % 2, 0:16].astype(F32)
        gains[0:2, i * 128 : (i + 1) * 128] = small[0:2]

    def unit(u):
        return ScatterW(
            net, ROWS_M, lambda yy: sums.at[u, yy], lambda yy: stage.at[u % 2, yy], far_m.at[u], near_m.at[u]
        )

    scatter = [unit(u) for u in range(6)]
    z_copies = [[] for _ in range(3)]

    staged = []

    def bring(u):
        to_core[u].wait_recv()
        staged.append(net.move(theirs_hbm.at[u], stage.at[u % 2]))

    def step_a(u):
        if u < 2:
            to_core[u].wait_recv()
        else:
            staged[u - 2].wait()
        load_sums[u].wait()
        scatter[u].step_a()
        if u < 4:
            bring(u + 2)

    def step_b(u):
        scatter[u].step_b()

    def step_c(u):
        k, flip = units[u]
        scatter[u].step_c()
        if flip:
            z_copies[k].append(net.send(sums.at[u, y, zh], by_z.at[k, 1], "zl"))
            z_copies[k].append(net.send(sums.at[u, y, 1 - zh], by_z.at[k, 2], "zo"))
        else:
            z_copies[k].append(net.send(sums.at[u, y, 1 - zh], by_z.at[k, 0], "zh"))

    def step_d(k):
        for copy in z_copies[k]:
            copy.wait_recv()

        total = sums[2 * k + 1, y, zh].astype(F32)
        for j in range(3):
            total = total + by_z[k, j].astype(F32)
        dm_ref[k] = total

    def attended_back(side):
        given = gb[pl.ds(side * 4, 4)].reshape(512, 2048)
        weight = jnp.concatenate([wa[i // 4, i // 2 % 2, i % 2, 784:1040] for i in range(16)], axis=1)
        value = nt(given, weight).astype(BF16)
        for i in range(4):
            ga[pl.ds(pl.multiple_of((2 * i + side) * 128, 128), 128)] = value[i * 128 : (i + 1) * 128]

    step_a(0)
    gather.relay()
    gather.relay_z()
    step_a(1)
    step_b(0)
    gather.relay_far()
    step_a(2)
    gather.plane()
    attended_back(net.zl)
    step_a(3)
    step_b(1)
    gather.rest()
    attended_back(1 - net.zl)
    load_down.wait()
    sum4 = ScatterX(net, down, got4, got4_half)
    sum4.start_far()
    sum4.start_near()
    for copy in load_rest:
        copy.wait()
    dk[...] = jnp.zeros_like(dk)
    dv[...] = jnp.zeros_like(dv)

    def attention_back(block):
        first, stop = block * 256, (block + 1) * 256
        q_block = q_ref[first:stop] * jnp.asarray(SCALE, BF16)
        ga_block = ga[first:stop]
        begin = begin_ref[first:stop, 0:1]
        dq = jnp.zeros((256, 256), F32)
        many_q, many_g, many_p, many_s = [], [], [], []
        for h in range(4):
            mask = head_mask(h)
            g_head = jnp.where(mask, ga_block, jnp.zeros_like(ga_block))
            scores = scores_of(q_block, k_ref[0:stop], begin, first, h)
            weights = jnp.exp(scores - jnp.max(scores, axis=-1, keepdims=True))
            probs = weights * (1.0 / jnp.sum(weights, axis=-1, keepdims=True))
            g_probs = nt(g_head, v_ref[0:stop])
            inner = jnp.sum(probs * g_probs, axis=-1, keepdims=True)
            g_scores = (probs * (g_probs - inner)).astype(BF16)
            dq = jnp.where(mask, nn(g_scores, k_ref[0:stop]), dq)
            many_q.append(jnp.where(mask, q_block, jnp.zeros_like(q_block)))
            many_g.append(g_head)
            many_p.append(probs.astype(BF16))
            many_s.append(g_scores)
        dk[0:stop] += tn(jnp.concatenate(many_s, axis=0), jnp.concatenate(many_q, axis=0))
        dv[0:stop] += tn(jnp.concatenate(many_p, axis=0), jnp.concatenate(many_g, axis=0))
        dq = turn(dq * SCALE, cos_ref[first:stop], sin_ref[first:stop], -1.0)
        gproj[first:stop, 0:256] = dq.astype(BF16)

    attention_back(0)
    attention_back(1)
    attention_back(2)
    attention_back(3)
    sum4.relay_near()

    def project_back(i, total):
        rows = pl.ds(pl.multiple_of(i * 128, 128), 128)
        d_key = turn(dk[rows], cos_ref[rows], sin_ref[rows], -1.0).astype(BF16)
        d_value = dv[rows].astype(BF16)
        gproj[rows, 256:512] = d_key
        gproj[rows, 512:768] = d_value
        row = [gproj[rows, 0:256].astype(F32), d_key.astype(F32), d_value.astype(F32)]
        return total + jnp.sum(jnp.concatenate(row, axis=1), axis=0, keepdims=True)

    bias = lax.fori_loop(0, 8, project_back, jnp.zeros((1, 768), F32))

    def normed_back(side):
        rows = [gproj[pl.ds(pl.multiple_of((2 * i + side) * 128, 128), 128)] for i in range(4)]
        rows = jnp.concatenate(rows, axis=0)
        for pair in range(8):
            weight = jnp.concatenate([wa[pair // 2, pair % 2, 0, 16:784], wa[pair // 2, pair % 2, 1, 16:784]], axis=1)
            part = nn(rows, weight).astype(BF16).reshape(4, 128, 256)
            parts[pl.ds(side * 4, 4), :, pair * 256 : (pair + 1) * 256] = part

    sum8 = ScatterTp(net, parts, got8, got8_half)
    normed_back(1 - net.zl)
    sum8.start_side()
    step_a(4)
    sum4.wait()
    load_middle.wait()
    out_ref[...] = (dtok_ref[...] + sum4.total()).astype(BF16)
    net.settle([sum4.half_p, sum4.half_m] + sum4.near_p + sum4.near_m)
    normed_back(net.zl)
    sum8.start_plane()
    step_c(0)
    step_b(2)
    step_a(5)
    step_c(1)
    step_b(3)
    step_c(2)
    for slot in range(8):
        chunk = slot % 4 * 2 + slot // 4
        flipped[0:256, slot * 128 : (slot + 1) * 128] = att_ref[chunk * 128 : (chunk + 1) * 128].T
    for pair in range(8):
        some = gb[:, :, pair * 256 : (pair + 1) * 256].reshape(1024, 256)
        product = nn(flipped[0:256], some).astype(BF16)
        wa[pair // 2, pair % 2, 0, 784:1040] = product[:, 0:128]
        wa[pair // 2, pair % 2, 1, 784:1040] = product[:, 128:256]
    net.settle([gather.zb_p, gather.zb_m, gather.fwd_p, gather.fwd_m, gather.za_p, gather.za_m, gather.fz_p, gather.fz_m])
    load_normed = net.move(normed_hbm, gb)
    sum8.relay_side()
    flipped[...] = gproj[...].T
    load_normed.wait()
    for pair in range(8):
        some = gb[:, :, pair * 256 : (pair + 1) * 256].reshape(1024, 256)
        product = nn(flipped[...], some).astype(BF16)
        wa[pair // 2, pair % 2, 0, 16:784] = product[:, 0:128]
        wa[pair // 2, pair % 2, 1, 16:784] = product[:, 128:256]
    first_core = net.send(wa.at[:, :, 1 - core, pl.ds(16, 1024)], theirs_a, "c")
    scatter_q = [
        ScatterW(
            net, end - begin,
            lambda yy, begin=begin, end=end: wa.at[yy, :, core, pl.ds(16 + begin, end - begin)],
            lambda yy, begin=begin, end=end: theirs_a.at[yy, :, pl.ds(begin, end - begin)],
            far_a.at[:, :, pl.ds(begin // 2, (end - begin) // 2)], near_a.at[:, :, pl.ds(begin, end - begin)],
        )
        for begin, end in FIRST_PIECES
    ]
    sum8.relay_across()
    step_b(4)
    step_c(3)
    first_core.wait_recv()
    for piece in scatter_q:
        piece.step_a()
    sum8.relay_near()
    step_b(5)
    step_c(4)
    step_d(0)
    scatter_q[0].step_b()
    step_c(5)
    sum8.wait()
    given = sum8.total()
    grad, normed = norm_back(x_ref[...].astype(F32), given, gains[0:1])
    dtok_ref[...] = gmid_ref[...] + grad
    gain_sum = jnp.sum(given * normed, axis=0, keepdims=True)
    bias_sum = jnp.sum(given, axis=0, keepdims=True)
    bias_rows = jnp.concatenate([bias[:, i * 128 : (i + 1) * 128] for i in range(6)], axis=0)
    small_out[:, 4:10] = jnp.broadcast_to(bias_rows[None], (16, 6, 128))
    small_out[:, 10:16] = jnp.zeros((16, 6, 128), F32)
    for i in range(16):
        lanes = slice(i * 128, (i + 1) * 128)
        small_out[i, 0:1] = gain_sum[:, lanes]
        small_out[i, 1:2] = bias_sum[:, lanes]
        small_out[i, 2:4] = ln2_ref[0:2, lanes]
    copies = [
        net.send(small_out.at[place[0]], small_in.at[i], place) for i, place in enumerate(across_f)
    ]
    scatter_q[1].step_b()
    z_q = []
    for piece, (begin, end) in zip(scatter_q, FIRST_PIECES):
        piece.step_c()
        lines = pl.ds(begin, end - begin)
        z_q.append(net.send(wa.at[y, 1 - zh, core, pl.ds(16 + begin, end - begin)], by_z_a.at[lines], "zh"))
    step_d(1)
    step_d(2)
    total = small_out[f]
    for i, copy in enumerate(copies):
        copy.wait_recv()
        total = total + small_in[i]
    small_tp[...] = total
    copies = [net.send(small_tp.at[pl.ds(0, 8)], small_got.at[j], place) for j, place in enumerate(across_t)]
    for copy in z_q:
        copy.wait_recv()

    da_ref[...] = wa[y, zh, core, pl.ds(16, 1024)].astype(F32) + by_z_a[...].astype(F32)
    row_id = lax.broadcasted_iota(jnp.int32, (8, 128), 0)
    total = small_tp[0:8]
    for j, copy in enumerate(copies):
        copy.wait_recv()
        total = total + jnp.where(row_id < 4, small_got[j], 0.0)
    small_ref[0:8] = total
    small_ref[8:16] = small_tp[8:16]
    net.finish()


def k3(x, lens, wa, gmid, middle, down, ln2, grads, normed, q, k, v, att):
    shapes = [
        ((128, 2048), BF16, VM), ((128, 2048), F32, VM), ((3, ROWS_M, 128), F32, VM), ((1024, 128), F32, VM),
        ((16, 128), F32, VM), ((6, 4, 2, ROWS_M, 128), BF16, AN),
    ]
    scratch = [
        ((1024, 256), BF16), ((1024, 256), BF16), ((1024, 256), BF16), ((1024, 256), BF16),
        ((4, 2, 2, ROWS_A, 128), BF16), ((8, 128, 2048), BF16), ((8, 128, 2048), BF16), ((3, 128, 2048), BF16),
        ((8, 64, 2048), BF16), ((2, 128, 2048), BF16), ((2, 64, 2048), BF16),
        ((128, 2048), BF16), ((8, 2048), F32), ((1024, 256), BF16), ((1024, 256), F32), ((1024, 256), F32),
        ((1024, 768), BF16), ((768, 1024), BF16), ((1024, 128), jnp.int32), ((1024, 128), F32), ((1024, 128), F32),
        ((6, 4, 2, ROWS_M, 128), BF16), ((2, 4, 2, ROWS_M, 128), BF16), ((6, 2, 2, ROWS_M // 2, 128), BF16),
        ((6, 2, 2, ROWS_M, 128), BF16), ((3, 3, ROWS_M, 128), BF16), ((4, 2, 1024, 128), BF16),
        ((2, 2, 512, 128), BF16), ((2, 2, 1024, 128), BF16),
        ((1024, 128), BF16), ((16, 16, 128), F32), ((15, 16, 128), F32), ((16, 128), F32), ((7, 8, 128), F32),
    ]
    return pl.pallas_call(
        k3_kernel,
        out_shape=[jax.ShapeDtypeStruct(s, d) for s, d, _ in shapes],
        in_specs=[VM, SM, AN, VM, AN, AN, VM, AN, AN, AN, AN, AN, AN],
        out_specs=[m for _, _, m in shapes],
        scratch_shapes=[pltpu.VMEM(s, d) for s, d in scratch]
        + [pltpu.SemaphoreType.DMA((160,)), pltpu.SemaphoreType.DMA((160,)), pltpu.SemaphoreType.DMA((24,))],
        compiler_params=pltpu.CompilerParams(
            collective_id=3, has_side_effects=True, vmem_limit_bytes=63 * MIB
        ),
        name="attend_back_sum_gradients",
    )(
        x, lens, wa.reshape(4, 2, 2, ROWS_A, 128), gmid, middle, down, ln2,
        grads.reshape(3, 2, 4, 2, 2, ROWS_M, 128), normed, q, k, v, att,
    )


def finish_kernel(
    out_in, dtok_in, dm_in, da_in, small_in,
    out_ref, dtok_ref, gain1, bias1, dqkv, dout, gain2, bias2, dgate, dup, ddown,
):
    out_ref[...] = out_in[...]
    dtok_ref[...] = dtok_in[...]
    for i, ref in enumerate((gain1, bias1, gain2, bias2)):
        ref[...] = small_in[i : i + 1]
    for j in range(3):
        for part in range(2):
            lanes = slice(part * 128, (part + 1) * 128)
            dqkv[j, :, lanes] = da_in[j * 256 + part * 128 : j * 256 + (part + 1) * 128].T
    dout[...] = da_in[768:1024]
    dgate[...] = dm_in[0]
    dup[...] = dm_in[1]
    ddown[...] = dm_in[2]


def finish(out, d_tokens, dm, da, small):
    shapes = [
        ((128, 2048), BF16), ((128, 2048), F32), ((1, 128), F32), ((1, 128), F32), ((3, 128, 256), F32), ((256, 128), F32),
        ((1, 128), F32), ((1, 128), F32), ((ROWS_M, 128), F32), ((ROWS_M, 128), F32), ((ROWS_M, 128), F32),
    ]
    return pl.pallas_call(
        finish_kernel,
        out_shape=[jax.ShapeDtypeStruct(s, d) for s, d in shapes],
        in_specs=[VM] * 5,
        out_specs=[VM] * 11,
        compiler_params=pltpu.CompilerParams(vmem_limit_bytes=63 * MIB),
        name="lay_out_gradients",
    )(out, d_tokens, dm, da, small)


def local(
    tokens, seq_lens, ln1_gain, ln1_bias, w_qkv, b_qkv, w_out, ln2_gain, ln2_bias, w_gate, w_up, w_down, cotangent
):
    small = small_rows(ln1_gain, ln1_bias, b_qkv, ln2_gain, ln2_bias)
    normed, wa, wg, cotg, q, k, v, att = k1(
        tokens, seq_lens, small, jnp.transpose(w_qkv, (1, 0, 2)), w_out, w_gate.T, cotangent
    )
    middle, gmid, down, grads, ln2 = k2(tokens, att, wa, wg, w_up.T, w_down, cotangent, cotg)
    out, d_tokens, dm, da, small, _ = k3(
        tokens, seq_lens, wa, gmid, middle, down, ln2, grads, normed, q, k, v, att
    )
    d_bias = lax.dynamic_slice_in_dim(
        small[4:10].reshape(3, 4, HEAD_DIM), lax.axis_index("fsdp") * 4, 4, axis=2
    )
    out, d_tokens, gain1, bias1, dqkv, dout, gain2, bias2, dgate, dup, ddown = finish(out, d_tokens, dm, da, small)
    return (
        out, d_tokens, gain1[0], bias1[0], jnp.transpose(dqkv, (1, 0, 2)), d_bias, dout, gain2[0], bias2[0], dgate.T, dup.T, ddown,
    )


def solution(mesh):
    placed = (
        P(("fsdp", "tp"), None),
        P("fsdp", None),
        P("fsdp"),
        P("fsdp"),
        P("fsdp", None, "tp"),
        P(None, "tp", "fsdp"),
        P("tp", "fsdp"),
        P("fsdp"),
        P("fsdp"),
        P("fsdp", "tp"),
        P("fsdp", "tp"),
        P("tp", "fsdp"),
        P(("fsdp", "tp"), None),
    )
    return jax.shard_map(
        local,
        mesh=mesh,
        in_specs=placed,
        out_specs=(
            P(("fsdp", "tp"), None),
            P(("fsdp", "tp"), None),
            P("fsdp"),
            P("fsdp"),
            P("fsdp", None, "tp"),
            P(None, "tp", "fsdp"),
            P("tp", "fsdp"),
            P("fsdp"),
            P("fsdp"),
            P("fsdp", "tp"),
            P("fsdp", "tp"),
            P("tp", "fsdp"),
        ),
        check_vma=False,
    )
```
